32 devices in a mesh: head: 4 (over x, core), wide: 8 (over z, y).
Axes of the slice: x: 2, y: 2, z: 4, core: 2. Of those that a mesh axis runs over, the one named last changes fastest.
Arguments:
- tokens: bfloat16 [8192, 2048], P(('wide', 'head')), may hold values from -6 to 6
- cotangent: bfloat16 [8192, 2048], P(('wide', 'head')), may hold values from -6 to 6
- segment_ids: int32 [8192], P('wide'), may hold values from 0 to 31, as said below
- domain_ids: int32 [8192], P(('wide', 'head')), may hold values from 0 to 7, as said below
- domain_weights: float32 [8], replicated, may hold values from 0.5 to 2
- gains: float32 [4352], replicated, may hold values from 0.5 to 1.7
- gain_first: float32 [4352], replicated, may hold values from -0.00036621094 to 0.00036621094
- gain_second: float32 [4352], replicated, may hold values from 8.339221e-09 to 1.3303043e-07
- query_weight: float32 [2048, 2048], P('wide', 'head'), may hold values from -0.125 to 0.125
- query_first: float32 [2048, 2048], P('wide', 'head'), may hold values from -9.1552734e-05 to 9.1552734e-05
- query_second: float32 [2048, 2048], P('wide', 'head'), may hold values from 5.2219407e-10 to 8.339221e-09
- keyvalue_weight: float32 [2, 2048, 1024], P(None, 'wide', 'head'), may hold values from -0.125 to 0.125
- keyvalue_first: float32 [2, 2048, 1024], P(None, 'wide', 'head'), may hold values from -9.1552734e-05 to 9.1552734e-05
- keyvalue_second: float32 [2, 2048, 1024], P(None, 'wide', 'head'), may hold values from 5.2219407e-10 to 8.339221e-09
- headgate_weight: float32 [2048, 16], P('wide', 'head'), may hold values from -0.125 to 0.125
- headgate_first: float32 [2048, 16], P('wide', 'head'), may hold values from -9.1552734e-05 to 9.1552734e-05
- headgate_second: float32 [2048, 16], P('wide', 'head'), may hold values from 5.2219407e-10 to 8.339221e-09
- output_weight: float32 [2048, 2048], P('head', 'wide'), may hold values from -1 to 1
- output_first: float32 [2048, 2048], P('head', 'wide'), may hold values from -7.6293945e-06 to 7.6293945e-06
- output_second: float32 [2048, 2048], P('head', 'wide'), may hold values from 8.1490726e-12 to 3.259629e-11
- expand_weight: float32 [2, 2048, 6144], P(None, 'head', 'wide'), may hold values from -0.125 to 0.125
- expand_first: float32 [2, 2048, 6144], P(None, 'head', 'wide'), may hold values from -9.1552734e-05 to 9.1552734e-05
- expand_second: float32 [2, 2048, 6144], P(None, 'head', 'wide'), may hold values from 5.2219407e-10 to 8.339221e-09
- reduce_weight: float32 [6144, 2048], P('wide', 'head'), may hold values from -0.078125 to 0.078125
- reduce_first: float32 [6144, 2048], P('wide', 'head'), may hold values from -9.1552734e-05 to 9.1552734e-05
- reduce_second: float32 [6144, 2048], P('wide', 'head'), may hold values from 5.2219407e-10 to 8.339221e-09
Outputs:
- grad_norm: float32 [], replicated
- block_output: bfloat16 [8192, 2048], P(('wide', 'head'))
- input_grad: float32 [8192, 2048], P(('wide', 'head'))
- updated_gains: float32 [4352], replicated
- first_gains: float32 [4352], replicated
- second_gains: float32 [4352], replicated
- updated_query: float32 [2048, 2048], P('wide', 'head')
- first_query: float32 [2048, 2048], P('wide', 'head')
- second_query: float32 [2048, 2048], P('wide', 'head')
- copied_query: bfloat16 [2048, 2048], P('wide', 'head')
- updated_keyvalue: float32 [2, 2048, 1024], P(None, 'wide', 'head')
- first_keyvalue: float32 [2, 2048, 1024], P(None, 'wide', 'head')
- second_keyvalue: float32 [2, 2048, 1024], P(None, 'wide', 'head')
- copied_keyvalue: bfloat16 [2, 2048, 1024], P(None, 'wide', 'head')
- updated_headgate: float32 [2048, 16], P('wide', 'head')
- first_headgate: float32 [2048, 16], P('wide', 'head')
- second_headgate: float32 [2048, 16], P('wide', 'head')
- copied_headgate: bfloat16 [2048, 16], P('wide', 'head')
- updated_output: float32 [2048, 2048], P('head', 'wide')
- first_output: float32 [2048, 2048], P('head', 'wide')
- second_output: float32 [2048, 2048], P('head', 'wide')
- copied_output: bfloat16 [2048, 2048], P('head', 'wide')
- updated_expand: float32 [2, 2048, 6144], P(None, 'head', 'wide')
- first_expand: float32 [2, 2048, 6144], P(None, 'head', 'wide')
- second_expand: float32 [2, 2048, 6144], P(None, 'head', 'wide')
- copied_expand: bfloat16 [2, 2048, 6144], P(None, 'head', 'wide')
- updated_reduce: float32 [6144, 2048], P('wide', 'head')
- first_reduce: float32 [6144, 2048], P('wide', 'head')
- second_reduce: float32 [6144, 2048], P('wide', 'head')
- copied_reduce: bfloat16 [6144, 2048], P('wide', 'head')
The draws below stay inside these ranges and needn't reach their ends.
Inputs may be any that keep to these rules, and one draw needn't show every extreme that they name: `segment_ids`: segment ids never fall along the tokens, and no segment crosses the border between two packed rows of 1024 tokens. `domain_ids`: all tokens of one segment have the same domain.
All inputs are finite; a program needn't handle non-finite values.
Results may differ from the reference program's by a relative error of at most 0.022.
Values may be sent and summed in bfloat16 or wider, within the bound.
No kernel may reach another device: no remote copies, remote signals or barrier semaphores. Data moves between devices by JAX's collectives and lax.ppermute only.
A program may use at most 320 MiB of HBM per device.

```python
import math
import jax
import jax.numpy as jnp
from jax import lax

D = 2048
H = 16
HD = 128
KVH = 8
FF = 6144
NDOM = 8
STEP = 10
GROUP = 1024
ROWS = 256
TOKENS = 8192
GAIN_COUNT = 4352


def layout(key):
    row_groups = TOKENS // GROUP
    keys = jax.random.split(key, 3)
    edge = max(ROWS // 2, 1) + 1
    head_len = jax.random.randint(keys[0], (row_groups,), 1, edge)
    tail_len = jax.random.randint(keys[1], (row_groups,), 1, edge)
    tail_cut = jax.random.randint(keys[2], (row_groups,), 0, 1 << 20) % tail_len
    places = jnp.arange(GROUP, dtype=jnp.int32)[None, :]
    local = (places >= head_len[:, None]).astype(jnp.int32)
    local = local + (places >= GROUP - tail_len[:, None]).astype(jnp.int32)
    local = local + (places >= GROUP - tail_len[:, None] + tail_cut[:, None]).astype(jnp.int32)
    return local


def draw_segment_ids(key, part):
    local = layout(key)
    row_groups = TOKENS // GROUP
    offsets = 4 * jnp.arange(row_groups, dtype=jnp.int32)[:, None]
    return (local + offsets).reshape(TOKENS)


def draw_domain_ids(key, part):
    local = layout(key)
    key = jax.random.fold_in(key, 5)
    row_groups = TOKENS // GROUP
    table = jax.random.randint(key, (row_groups, 4), 0, NDOM)
    table = table.at[0, 0].set(0).at[0, 3].set(NDOM - 1)
    return jnp.take_along_axis(table, local, 1).reshape(TOKENS)


def draw_gains(key, part):
    key = jax.random.fold_in(key, 11)
    first_key, second_key = jax.random.split(key)
    places = jnp.arange(D, dtype=jnp.float32) / D
    ramp = 0.75 + 0.55 * places
    spread = jax.random.uniform(first_key, (2, D), minval=0.8, maxval=1.25)
    heads = jax.random.uniform(second_key, (2 * HD,), minval=0.7, maxval=1.4)
    return jnp.concatenate([(ramp[None, :] * spread).reshape(2 * D), heads])


def shard_levels(rng, shape, shards, low, high):
    level = 1.0
    for axis_at, parts in shards:
        heights = jax.random.uniform(jax.random.fold_in(jax.random.fold_in(rng, 6), axis_at), (parts,), jnp.float32, low / len(shards), high / len(shards))
        level = level * jnp.repeat(jnp.exp(heights), shape[axis_at] // parts).reshape((-1,) + (1,) * (len(shape) - 1 - axis_at))
    return level


def noise(stream_key, dims, deviation, most, pieces=(), held_as=jnp.bfloat16):
    entries = deviation * jax.random.normal(stream_key, dims, jnp.float32)
    if pieces:
        entries = entries * shard_levels(stream_key, dims, pieces, -0.22, 0.18)
    return jnp.clip(entries, -most, most).astype(held_as)


def setup_inputs(seed: int = 0) -> dict:
    key_list = jax.random.split(jax.random.key(seed), 27)
    tokens = noise(key_list[0], (TOKENS, D), 1.0, 6.0, ((0, 32),))
    cotangent = noise(key_list[1], (TOKENS, D), 1.0, 6.0, ((0, 32),))
    segment_ids = draw_segment_ids(jax.random.fold_in(key_list[26], 71), 0)
    domain_ids = draw_domain_ids(jax.random.fold_in(key_list[26], 71), 0)
    domain_weights = jnp.clip(jnp.exp(jax.random.uniform(key_list[4], (NDOM,), jnp.float32, math.log(0.5), math.log(2.0))), 0.5, 2.0)
    gains = draw_gains(jax.random.fold_in(key_list[26], 71), 0)
    gain_first = noise(key_list[6], (GAIN_COUNT,), (0.444 * (2 * D * H * HD + 2 * D * KVH * HD + D * H + 3 * D * FF) ** -0.5), 0.00036621094, (), jnp.float32)
    gain_second = jnp.clip(jnp.exp(jax.random.uniform(key_list[7], (GAIN_COUNT,), jnp.float32, math.log(8.339220869402197e-09), math.log(1.3303042578627355e-07))), 8.339220869402197e-09, 1.3303042578627355e-07)
    query_weight = noise(key_list[8], (D, H * HD), D ** -0.5, 0.125, ((0, 8), (1, 4)), jnp.float32)
    query_first = noise(key_list[9], (D, H * HD), (0.111 * (2 * D * H * HD + 2 * D * KVH * HD + D * H + 3 * D * FF) ** -0.5), 9.1552734375e-05, ((0, 8), (1, 4)), jnp.float32)
    query_second = jnp.clip(jnp.exp(math.log(8.339220869402197e-09) - 2.77068578 * jax.random.uniform(key_list[10], (D, H * HD), jnp.float32) ** shard_levels(key_list[10], (D, H * HD), ((0, 8), (1, 4)), -0.2, 0.2)), 5.221940657662572e-10, 8.339220869402197e-09)
    keyvalue_weight = noise(key_list[11], (2, D, KVH * HD), D ** -0.5, 0.125, ((1, 8), (2, 4)), jnp.float32)
    keyvalue_first = noise(key_list[12], (2, D, KVH * HD), (0.111 * (2 * D * H * HD + 2 * D * KVH * HD + D * H + 3 * D * FF) ** -0.5), 9.1552734375e-05, ((1, 8), (2, 4)), jnp.float32)
    keyvalue_second = jnp.clip(jnp.exp(math.log(8.339220869402197e-09) - 2.77068578 * jax.random.uniform(key_list[13], (2, D, KVH * HD), jnp.float32) ** shard_levels(key_list[13], (2, D, KVH * HD), ((1, 8), (2, 4)), -0.2, 0.2)), 5.221940657662572e-10, 8.339220869402197e-09)
    headgate_weight = noise(key_list[14], (D, H), D ** -0.5, 0.125, ((0, 8), (1, 4)), jnp.float32)
    headgate_first = noise(key_list[15], (D, H), (0.111 * (2 * D * H * HD + 2 * D * KVH * HD + D * H + 3 * D * FF) ** -0.5), 9.1552734375e-05, ((0, 8), (1, 4)), jnp.float32)
    headgate_second = jnp.clip(jnp.exp(math.log(8.339220869402197e-09) - 2.77068578 * jax.random.uniform(key_list[16], (D, H), jnp.float32) ** shard_levels(key_list[16], (D, H), ((0, 8), (1, 4)), -0.2, 0.2)), 5.221940657662572e-10, 8.339220869402197e-09)
    output_weight = noise(key_list[17], (H * HD, D), (H * HD // 64) ** -0.5, 1.0, ((0, 4), (1, 8)), jnp.float32)
    output_first = noise(key_list[18], (H * HD, D), (0.157 * (GROUP * D * FF) ** -0.5), 7.62939453125e-06, ((0, 4), (1, 8)), jnp.float32)
    output_second = jnp.clip(jnp.exp(math.log(3.2596290250319626e-11) - 1.3862944 * jax.random.uniform(key_list[19], (H * HD, D), jnp.float32) ** shard_levels(key_list[19], (H * HD, D), ((0, 4), (1, 8)), -0.2, 0.2)), 8.149072562579907e-12, 3.2596290250319626e-11)
    expand_weight = noise(key_list[20], (2, D, FF), D ** -0.5, 0.125, ((1, 4), (2, 8)), jnp.float32)
    expand_first = noise(key_list[21], (2, D, FF), (0.111 * (2 * D * H * HD + 2 * D * KVH * HD + D * H + 3 * D * FF) ** -0.5), 9.1552734375e-05, ((1, 4), (2, 8)), jnp.float32)
    expand_second = jnp.clip(jnp.exp(math.log(8.339220869402197e-09) - 2.77068578 * jax.random.uniform(key_list[22], (2, D, FF), jnp.float32) ** shard_levels(key_list[22], (2, D, FF), ((1, 4), (2, 8)), -0.2, 0.2)), 5.221940657662572e-10, 8.339220869402197e-09)
    reduce_weight = noise(key_list[23], (FF, D), FF ** -0.5, 0.078125, ((0, 8), (1, 4)), jnp.float32)
    reduce_first = noise(key_list[24], (FF, D), (0.111 * (2 * D * H * HD + 2 * D * KVH * HD + D * H + 3 * D * FF) ** -0.5), 9.1552734375e-05, ((0, 8), (1, 4)), jnp.float32)
    reduce_second = jnp.clip(jnp.exp(math.log(8.339220869402197e-09) - 2.77068578 * jax.random.uniform(key_list[25], (FF, D), jnp.float32) ** shard_levels(key_list[25], (FF, D), ((0, 8), (1, 4)), -0.2, 0.2)), 5.221940657662572e-10, 8.339220869402197e-09)
    return dict(tokens=tokens, cotangent=cotangent, segment_ids=segment_ids, domain_ids=domain_ids, domain_weights=domain_weights, gains=gains, gain_first=gain_first, gain_second=gain_second, query_weight=query_weight, query_first=query_first, query_second=query_second, keyvalue_weight=keyvalue_weight, keyvalue_first=keyvalue_first, keyvalue_second=keyvalue_second, headgate_weight=headgate_weight, headgate_first=headgate_first, headgate_second=headgate_second, output_weight=output_weight, output_first=output_first, output_second=output_second, expand_weight=expand_weight, expand_first=expand_first, expand_second=expand_second, reduce_weight=reduce_weight, reduce_first=reduce_first, reduce_second=reduce_second)


@jax.custom_vjp
def low(v):
    return lax.optimization_barrier(v.astype(jnp.bfloat16)).astype(jnp.float32)

@jax.custom_vjp
def low_back(v):
    return v

def low_keep(v):
    return (low(v), None)

def low_pass(kept, grad):
    return (grad,)

def back_keep(v):
    return (v, None)

def back_low(kept, grad):
    return (low(grad),)
low.defvjp(low_keep, low_pass)
low_back.defvjp(back_keep, back_low)
NORM_EPS = 1e-06
ROPE_BASE = 1000000.0
MASK_FILL = -1e+30
CLIP_NORM = 1.0
WEIGHT_RATE = 0.02
OUTPUT_RATE = 0.12
GAIN_RATE = 0.7
BETA_FIRST = 0.9
BETA_SECOND = 0.95
ADAM_EPS = 1e-08
WEIGHT_DECAY = 0.1
HIGHEST = lax.Precision.HIGHEST

def matmul(left, right):
    return jnp.dot(left, right, precision=HIGHEST, preferred_element_type=jnp.float32)

def rms_scale(values):
    return values * lax.rsqrt(lax.optimization_barrier(jnp.mean(values * values, -1, keepdims=True)) + NORM_EPS)

def positions(segments):
    length = segments.shape[0]
    places = jnp.arange(length, dtype=jnp.int32)
    starts = jnp.concatenate([jnp.ones((1,), dtype=bool), segments[1:] != segments[:-1]])
    return places - lax.cummax(jnp.where(starts, places, 0), axis=0)

def rotate(values, places):
    half = values.shape[-1] // 2
    freqs = ROPE_BASE ** (-2.0 * jnp.arange(half, dtype=jnp.float32) / values.shape[-1])
    angles = places.astype(jnp.float32)[:, None] * freqs[None, :]
    cosine = jnp.cos(angles)[:, None, :]
    sine = jnp.sin(angles)[:, None, :]
    first_half = values[..., :half]
    second_half = values[..., half:]
    return jnp.concatenate([first_half * cosine - second_half * sine, second_half * cosine + first_half * sine], -1)

def head_prep(raw, gain, places):
    shaped = raw.reshape(raw.shape[0], -1, gain.shape[0])
    return rotate(rms_scale(shaped) * gain, places)

def attend(query_rot, key_rot, value_low, segments):
    length = query_rot.shape[0]
    block_size = min(512, length)
    block_count = length // block_size
    repeat = H // KVH
    query_blocks = query_rot.reshape(block_count, block_size, KVH, repeat, HD)
    block_starts = jnp.arange(block_count, dtype=jnp.int32) * block_size
    key_places = jnp.arange(length, dtype=jnp.int32)

    def one_block(args):
        query_block, start = args
        raw_scores = jnp.einsum('qgrd,kgd->grqk', query_block, key_rot, precision=HIGHEST) * HD ** (-0.5)
        scores = low_back(raw_scores)
        query_places = start + jnp.arange(block_size, dtype=jnp.int32)
        query_segments = lax.dynamic_slice_in_dim(segments, start, block_size)
        allowed = (key_places[None, :] <= query_places[:, None]) & (segments[None, :] == query_segments[:, None])
        scores = jnp.where(allowed, scores, MASK_FILL)
        largest = lax.optimization_barrier(jnp.max(scores, -1, keepdims=True))
        exponent = jnp.exp(scores - largest)
        probs = low(exponent / lax.optimization_barrier(jnp.sum(exponent, -1, keepdims=True)))
        attended = jnp.einsum('grqk,kgd->qgrd', probs, value_low, precision=HIGHEST)
        return low_back(attended)
    outs = lax.map(jax.checkpoint(one_block), (query_blocks, block_starts))
    return outs.reshape(length, H, HD)

def layer(lowered, gains, inputs, segments):
    query_low, keyvalue_low, headgate_low, output_low, expand_low, reduce_low = lowered
    length = inputs.shape[0]
    norm_one = gains[:D]
    norm_two = gains[D:2 * D]
    query_gain = gains[2 * D:2 * D + HD]
    key_gain = gains[2 * D + HD:]
    places = positions(segments)
    normed = low(rms_scale(inputs) * norm_one)
    query = low_back(matmul(normed, query_low))
    key = low_back(matmul(normed, keyvalue_low[0]))
    value = low(low_back(matmul(normed, keyvalue_low[1])))
    gate_logit = low_back(matmul(normed, headgate_low))
    query_rot = low(head_prep(query, query_gain, places))
    key_rot = low(head_prep(key, key_gain, places))
    attended = attend(query_rot, key_rot, value.reshape(length, KVH, HD), segments)
    gated = low((attended * jax.nn.sigmoid(gate_logit)[:, :, None]).reshape(length, H * HD))
    residual = inputs + low_back(matmul(gated, output_low))
    mixed = low(rms_scale(residual) * norm_two)
    gate_pre = low_back(matmul(mixed, expand_low[0]))
    up_pre = low_back(matmul(mixed, expand_low[1]))
    activation = low(jax.nn.silu(gate_pre) * up_pre)
    return residual + low_back(matmul(activation, reduce_low))

def adam_step(weight, grad, first, second, rate, decay):
    first_new = BETA_FIRST * first + (1.0 - BETA_FIRST) * grad
    second_new = BETA_SECOND * second + (1.0 - BETA_SECOND) * grad * grad
    first_hat = first_new / (1.0 - BETA_FIRST ** STEP)
    second_hat = second_new / (1.0 - BETA_SECOND ** STEP)
    updated = weight - rate * (first_hat / (jnp.sqrt(second_hat) + ADAM_EPS) + decay * weight)
    return (updated, first_new, second_new)

def reference(tokens, cotangent, segment_ids, domain_ids, domain_weights, gains, gain_first, gain_second, query_weight, query_first, query_second, keyvalue_weight, keyvalue_first, keyvalue_second, headgate_weight, headgate_first, headgate_second, output_weight, output_first, output_second, expand_weight, expand_first, expand_second, reduce_weight, reduce_first, reduce_second):
    labels = jnp.arange(NDOM, dtype=jnp.int32)
    onehot = domain_ids[:, None] == labels[None, :]
    token_weight = lax.optimization_barrier(jnp.sum(jnp.where(onehot, domain_weights[None, :], 0.0), -1))
    upstream = cotangent.astype(jnp.float32) * token_weight[:, None]
    params = (query_weight, keyvalue_weight, headgate_weight, output_weight, expand_weight, reduce_weight, gains)
    row_groups = TOKENS // GROUP

    def forward(weights, inputs):
        lowered = tuple((low(weight) for weight in weights[:6]))

        def one_group(carry, args):
            return (carry, layer(lowered, weights[6], args[0], args[1]))
        stacked = inputs.reshape(row_groups, GROUP, D)
        seg_stack = segment_ids.reshape(row_groups, GROUP)
        _, outs = lax.scan(jax.checkpoint(one_group), jnp.zeros((), jnp.float32), (stacked, seg_stack))
        return outs.reshape(TOKENS, D)
    result, pullback = jax.vjp(forward, params, tokens.astype(jnp.float32))
    grads, input_grad = pullback(upstream)
    squares = jnp.zeros((), jnp.float32)
    for grad in grads:
        squares = squares + jnp.sum(grad * grad)
    grad_norm = jnp.sqrt(squares)
    clip = CLIP_NORM / jnp.maximum(grad_norm, CLIP_NORM)
    states = ((query_first, query_second), (keyvalue_first, keyvalue_second), (headgate_first, headgate_second), (output_first, output_second), (expand_first, expand_second), (reduce_first, reduce_second))
    gains_new = adam_step(gains, grads[6] * clip, gain_first, gain_second, GAIN_RATE, 0.0)
    outs = [grad_norm, result.astype(jnp.bfloat16), input_grad, gains_new[0], gains_new[1], gains_new[2]]
    for index in range(6):
        rate = OUTPUT_RATE if index == 3 else WEIGHT_RATE
        updated, first_new, second_new = adam_step(params[index], grads[index] * clip, states[index][0], states[index][1], rate, WEIGHT_DECAY)
        outs = outs + [updated, first_new, second_new, updated.astype(jnp.bfloat16)]
    return (outs[0], outs[1], outs[2], outs[3], outs[4], outs[5], outs[6], outs[7], outs[8], outs[9], outs[10], outs[11], outs[12], outs[13], outs[14], outs[15], outs[16], outs[17], outs[18], outs[19], outs[20], outs[21], outs[22], outs[23], outs[24], outs[25], outs[26], outs[27], outs[28], outs[29])
```

```python
import jax
import jax.numpy as jnp
from jax import lax
from jax.sharding import Mesh
from jax.sharding import PartitionSpec as P

D = 2048
H = 16
HD = 128
KVH = 8
NDOM = 8
STEP = 10


NORM_EPS = 1e-06
ROPE_BASE = 1000000.0
MASK_FILL = -1e30
CLIP_NORM = 1.0
WEIGHT_RATE = 0.02
OUTPUT_RATE = 0.12
GAIN_RATE = 0.7
BETA_FIRST = 0.9
BETA_SECOND = 0.95
ADAM_EPS = 1e-08
WEIGHT_DECAY = 0.1


def rms_scale(values):
    return values * lax.rsqrt(jnp.mean(values * values, -1, keepdims=True) + NORM_EPS)


def norm_rows(values, gain):
    return rms_scale(values) * gain


def positions(segments):
    length = segments.shape[0]
    places = jnp.arange(length, dtype=jnp.int32)
    starts = jnp.concatenate([jnp.ones((1,), dtype=bool), segments[1:] != segments[:-1]])
    return places - lax.cummax(jnp.where(starts, places, 0), axis=0)


def rotate(values, places):
    half = values.shape[-1] // 2
    freqs = ROPE_BASE ** (-2.0 * jnp.arange(half, dtype=jnp.float32) / values.shape[-1])
    angles = places.astype(jnp.float32)[:, None] * freqs[None, :]
    cosine = jnp.cos(angles)[:, None, :]
    sine = jnp.sin(angles)[:, None, :]
    first_half = values[..., :half]
    second_half = values[..., half:]
    return jnp.concatenate(
        [first_half * cosine - second_half * sine, second_half * cosine + first_half * sine], -1
    )


def head_prep(raw, gain, places):
    shaped = raw.reshape(raw.shape[0], -1, gain.shape[0])
    return rotate(rms_scale(shaped) * gain, places)


def contract_rows(left, right):
    return lax.dot_general(
        left, right, (((0,), (0,)), ((), ())), preferred_element_type=jnp.float32
    )


def contract_cols(left, right):
    return lax.dot_general(
        left, right, (((1,), (1,)), ((), ())), preferred_element_type=jnp.float32
    )


def swiglu_back(activation_grad, gate_pre, up_pre):
    gate_sigmoid = jax.nn.sigmoid(gate_pre)
    gate_grad = (
        activation_grad * up_pre * gate_sigmoid * (1.0 + gate_pre * (1.0 - gate_sigmoid))
    ).astype(jnp.bfloat16)
    up_grad = (activation_grad * gate_pre * gate_sigmoid).astype(jnp.bfloat16)
    return (gate_grad, up_grad)


def adam_step(weight, grad, first, second, rate, decay):
    first_new = BETA_FIRST * first + (1.0 - BETA_FIRST) * grad
    second_new = BETA_SECOND * second + (1.0 - BETA_SECOND) * grad * grad
    first_hat = first_new / (1.0 - BETA_FIRST**STEP)
    second_hat = second_new / (1.0 - BETA_SECOND**STEP)
    updated = weight - rate * (first_hat / (jnp.sqrt(second_hat) + ADAM_EPS) + decay * weight)
    return (updated, first_new, second_new)


def hop(value, axis):
    size = lax.axis_size(axis)
    return lax.ppermute(value, axis, [(i, (i - 1) % size) for i in range(size)])


def ring_gather(value, axis):
    pieces = [value]
    for _ in range(lax.axis_size(axis) - 1):
        pieces.append(hop(pieces[-1], axis))
    return pieces


def ring_scatter(parts, axis):
    size = lax.axis_size(axis)
    total = parts[1 % size]
    for step in range(1, size):
        total = parts[(step + 1) % size] + hop(total.astype(jnp.bfloat16), axis).astype(jnp.float32)
    return total


def all_sum(value, axis):
    pieces = ring_gather(value, axis)
    while len(pieces) > 1:
        half = len(pieces) // 2
        pieces = [pieces[i] + pieces[i + half] for i in range(half)]
    return pieces[0]


def rolled(values, shift, axis):
    size = values.shape[axis]
    return lax.dynamic_slice_in_dim(
        jnp.concatenate([values, values], axis), lax.rem(shift + size, size), size, axis
    )


def to_relative(values):
    rows, width = values.shape
    shaped = values.reshape(rows, lax.axis_size("a"), lax.axis_size("b"), -1)
    shaped = rolled(rolled(shaped, lax.axis_index("a"), 1), lax.axis_index("b"), 2)
    return shaped.reshape(rows, width)


def from_relative(values):
    rows, width = values.shape
    shaped = values.reshape(rows, lax.axis_size("a"), lax.axis_size("b"), -1)
    shaped = rolled(rolled(shaped, -lax.axis_index("a"), 1), -lax.axis_index("b"), 2)
    return shaped.reshape(rows, width)


def wide_gather(value):
    pieces = []
    for piece in ring_gather(value, "a"):
        pieces = pieces + ring_gather(piece, "b")
    return pieces


def wide_scatter(parts):
    inner = lax.axis_size("b")
    sums = []
    for i in range(lax.axis_size("a")):
        sums.append(ring_scatter(parts[i * inner : (i + 1) * inner], "b"))
    return ring_scatter(sums, "a")


def head_gather(value):
    rows, width = value.shape
    x_size = lax.axis_size("x")
    x_me, c_me = lax.axis_index("x"), lax.axis_index("c")
    result = jnp.zeros((x_size * 2 * rows, width), value.dtype)
    for i, piece in enumerate(ring_gather(value, "x")):
        for j, item in enumerate(ring_gather(piece, "c")):
            slot = lax.rem(x_me + i, x_size) * 2 + lax.rem(c_me + j, 2)
            result = lax.dynamic_update_slice(result, item, (slot * rows, 0))
    return result


def head_scatter(values, contract):
    x_size = lax.axis_size("x")
    x_me, c_me = lax.axis_index("x"), lax.axis_index("c")
    width = values.shape[-1]
    shaped = values.reshape(x_size, 2, -1, width)
    rows = shaped.shape[2]
    other = lax.dynamic_slice_in_dim(shaped, 1 - c_me, 1, 1).reshape(-1, width)
    mine = lax.dynamic_slice_in_dim(shaped, c_me, 1, 1).reshape(-1, width)
    received = lax.ppermute(contract(other).astype(jnp.bfloat16), "c", [(0, 1), (1, 0)])
    total = contract(mine) + received.astype(jnp.float32)
    parts = [
        lax.dynamic_slice_in_dim(total, lax.rem(x_me + i, x_size) * rows, rows, 0)
        for i in range(x_size)
    ]
    return ring_scatter(parts, "x")


def body(
    tokens,
    cotangent,
    segment_ids,
    domain_ids,
    domain_weights,
    gains,
    gain_first,
    gain_second,
    query_weight,
    query_first,
    query_second,
    keyvalue_weight,
    keyvalue_first,
    keyvalue_second,
    headgate_weight,
    headgate_first,
    headgate_second,
    output_weight,
    output_first,
    output_second,
    expand_weight,
    expand_first,
    expand_second,
    reduce_weight,
    reduce_first,
    reduce_second,
):
    head_devices = lax.axis_size("x") * lax.axis_size("c")
    outer, inner = lax.axis_size("a"), lax.axis_size("b")
    heads_local = H // head_devices
    groups_local = KVH // head_devices
    repeat = H // KVH
    labels = jnp.arange(NDOM, dtype=jnp.int32)
    onehot = domain_ids[:, None] == labels[None, :]
    token_weight = jnp.sum(jnp.where(onehot, domain_weights[None, :], 0.0), -1)
    upstream = cotangent.astype(jnp.float32) * token_weight[:, None]
    norm_one = gains[:D]
    norm_two = gains[D : 2 * D]
    query_gain = gains[2 * D : 2 * D + HD]
    key_gain = gains[2 * D + HD :]
    inputs = tokens.astype(jnp.float32)
    normed = norm_rows(inputs, norm_one).astype(jnp.bfloat16)
    group_in = lax.all_gather(to_relative(normed), ("x", "c"), axis=0, tiled=True)
    query_width, key_width = query_weight.shape[1], keyvalue_weight.shape[2]
    pad = -heads_local % 128
    low_weights = [
        query_weight,
        keyvalue_weight[0],
        keyvalue_weight[1],
        headgate_weight,
        jnp.zeros((query_weight.shape[0], pad), jnp.float32),
    ]
    project = jnp.concatenate(low_weights, 1).astype(jnp.bfloat16)
    project_all = jnp.concatenate(wide_gather(project), 0)
    output_all = jnp.concatenate(wide_gather(output_weight.astype(jnp.bfloat16)), 1)
    value_from = query_width + key_width
    gate_from = value_from + key_width
    expand_low = jnp.concatenate([expand_weight[0], expand_weight[1]], 1).astype(jnp.bfloat16)
    reduce_low = reduce_weight.astype(jnp.bfloat16)
    expand_all = [
        lax.all_gather(piece, ("x", "c"), axis=0, tiled=True)
        for piece in ring_gather(expand_low, "b")
    ]
    reduce_all = [
        lax.all_gather(piece, ("x", "c"), axis=1, tiled=True)
        for piece in ring_gather(reduce_low, "b")
    ]
    hidden = reduce_low.shape[0]
    upstream_parts = ring_gather(upstream.astype(jnp.bfloat16), "a")
    group_size = group_in.shape[0]
    places = positions(segment_ids)
    raw = jnp.dot(group_in, project_all, preferred_element_type=jnp.float32)
    query_raw = raw[:, :query_width]
    key_raw = raw[:, query_width:value_from]
    value_raw = raw[:, value_from:gate_from]
    gate_logit = raw[:, gate_from : gate_from + heads_local]
    query_rot = head_prep(query_raw, query_gain, places).astype(jnp.bfloat16)
    key_low = head_prep(key_raw, key_gain, places).astype(jnp.bfloat16)
    value_low = value_raw.astype(jnp.bfloat16).reshape(group_size, groups_local, HD)
    block_size = min(512, group_size)
    block_count = group_size // block_size
    key_places = jnp.arange(group_size, dtype=jnp.int32)
    score_scale = HD ** (-0.5)
    block_starts = jnp.arange(block_count, dtype=jnp.int32) * block_size
    query_blocks = query_rot.reshape(block_count, block_size, groups_local, repeat, HD)

    def masked_scores(query_block, start):
        raw_scores = (
            jnp.einsum("qgrd,kgd->grqk", query_block, key_low, preferred_element_type=jnp.float32)
            * score_scale
        )
        query_places = start + jnp.arange(block_size, dtype=jnp.int32)
        query_segments = lax.dynamic_slice_in_dim(segment_ids, start, block_size)
        allowed = (key_places[None, :] <= query_places[:, None]) & (
            segment_ids[None, :] == query_segments[:, None]
        )
        return jnp.where(allowed, raw_scores, MASK_FILL)

    def attend_block(args):
        query_block, start = args
        scores = masked_scores(query_block, start)
        largest = jnp.max(scores, -1, keepdims=True)
        exponent = jnp.exp(scores - largest)
        totals = jnp.sum(exponent, -1, keepdims=True)
        probs = (exponent / totals).astype(jnp.bfloat16)
        attended = jnp.einsum(
            "grqk,kgd->qgrd", probs, value_low, preferred_element_type=jnp.float32
        )
        return (attended, largest[..., 0] + jnp.log(totals[..., 0]))

    attended, log_totals = lax.map(attend_block, (query_blocks, block_starts))
    attended = attended.reshape(group_size, heads_local, HD)
    gate_sig = jax.nn.sigmoid(gate_logit)
    gated = (
        (attended * gate_sig[:, :, None]).reshape(group_size, heads_local * HD).astype(jnp.bfloat16)
    )
    residual = inputs + from_relative(
        head_scatter(
            gated, lambda rows: jnp.dot(rows, output_all, preferred_element_type=jnp.float32)
        )
    )
    mixed = norm_rows(residual, norm_two).astype(jnp.bfloat16)
    mixed_parts = ring_gather(mixed, "a")
    activations = [[] for _ in range(inner)]
    hidden_grads = [[] for _ in range(inner)]
    output_parts = []
    mixed_grad_parts = []
    for mixed_part, upstream_part in zip(mixed_parts, upstream_parts):
        output_sum = 0.0
        mixed_grad_sum = 0.0
        for j in range(inner):
            both = jnp.dot(mixed_part, expand_all[j], preferred_element_type=jnp.float32)
            gate_pre, up_pre = both[:, :hidden], both[:, hidden:]
            activation = (jax.nn.silu(gate_pre) * up_pre).astype(jnp.bfloat16)
            activation_grad = contract_cols(upstream_part, reduce_all[j])
            hidden_grad = jnp.concatenate(swiglu_back(activation_grad, gate_pre, up_pre), 1)
            output_sum = output_sum + jnp.dot(
                activation, reduce_all[j], preferred_element_type=jnp.float32
            )
            mixed_grad_sum = mixed_grad_sum + contract_cols(hidden_grad, expand_all[j])
            activations[j].append(activation)
            hidden_grads[j].append(hidden_grad)
        output_parts.append(output_sum)
        mixed_grad_parts.append(mixed_grad_sum)
    mixed_grad = ring_scatter(mixed_grad_parts, "a")
    block_output = (residual + ring_scatter(output_parts, "a")).astype(jnp.bfloat16)
    mixed_all = jnp.concatenate(mixed_parts, 0)
    upstream_all = jnp.concatenate(upstream_parts, 0)
    expand_parts = []
    reduce_parts = []
    for j in range(inner):
        expand_grad = contract_rows(mixed_all, jnp.concatenate(hidden_grads[j], 0))
        reduce_grad = contract_rows(jnp.concatenate(activations[j], 0), upstream_all)
        expand_parts.append(
            lax.psum_scatter(
                expand_grad.astype(jnp.bfloat16), ("x", "c"), scatter_dimension=0, tiled=True
            ).astype(jnp.float32)
        )
        reduce_parts.append(
            lax.psum_scatter(
                reduce_grad.astype(jnp.bfloat16), ("x", "c"), scatter_dimension=1, tiled=True
            ).astype(jnp.float32)
        )
    expand_both = ring_scatter(expand_parts, "b")
    expand_part = jnp.stack([expand_both[:, :hidden], expand_both[:, hidden:]])
    reduce_part = ring_scatter(reduce_parts, "b")
    _, second_back = jax.vjp(norm_rows, residual, norm_two)
    residual_from, two_grad = second_back(mixed_grad)
    residual_grad = upstream + residual_from
    residual_all = head_gather(to_relative(residual_grad.astype(jnp.bfloat16)))
    output_grad = contract_rows(gated, residual_all)
    gated_grad = contract_cols(residual_all, output_all).reshape(group_size, heads_local, HD)
    attended_grad = (gated_grad * gate_sig[:, :, None]).astype(jnp.bfloat16)
    logit_grad = (jnp.sum(gated_grad * attended, -1) * gate_sig * (1.0 - gate_sig)).astype(
        jnp.bfloat16
    )
    grad_blocks = attended_grad.reshape(block_count, block_size, groups_local, repeat, HD)

    def back_block(carry, args):
        key_sum, value_sum = carry
        query_block, grad_block, log_block, start = args
        scores = masked_scores(query_block, start)
        probs = jnp.exp(scores - log_block[..., None])
        prob_grad = jnp.einsum(
            "qgrd,kgd->grqk", grad_block, value_low, preferred_element_type=jnp.float32
        )
        inner = jnp.sum(probs * prob_grad, -1, keepdims=True)
        score_grad = (probs * (prob_grad - inner)).astype(jnp.bfloat16)
        query_grad = (
            jnp.einsum("grqk,kgd->qgrd", score_grad, key_low, preferred_element_type=jnp.float32)
            * score_scale
        )
        key_sum = (
            key_sum
            + jnp.einsum(
                "grqk,qgrd->kgd", score_grad, query_block, preferred_element_type=jnp.float32
            )
            * score_scale
        )
        value_sum = value_sum + jnp.einsum(
            "grqk,qgrd->kgd",
            probs.astype(jnp.bfloat16),
            grad_block,
            preferred_element_type=jnp.float32,
        )
        return ((key_sum, value_sum), query_grad)

    zeros = jnp.zeros((group_size, groups_local, HD), jnp.float32)
    (key_rot_grad, value_grad), query_grads = lax.scan(
        back_block, (zeros, zeros), (query_blocks, grad_blocks, log_totals, block_starts)
    )
    _, query_back = jax.vjp(lambda raw, gain: head_prep(raw, gain, places), query_raw, query_gain)
    query_raw_grad, query_gain_grad = query_back(query_grads.reshape(group_size, heads_local, HD))
    _, key_back = jax.vjp(lambda raw, gain: head_prep(raw, gain, places), key_raw, key_gain)
    key_raw_grad, key_gain_grad = key_back(key_rot_grad)
    query_low_grad = query_raw_grad.astype(jnp.bfloat16)
    key_low_grad = key_raw_grad.astype(jnp.bfloat16)
    value_low_grad = value_grad.reshape(group_size, groups_local * HD).astype(jnp.bfloat16)
    low_grads = jnp.concatenate(
        [
            query_low_grad,
            key_low_grad,
            value_low_grad,
            logit_grad,
            jnp.zeros((group_size, pad), jnp.bfloat16),
        ],
        1,
    )
    project_grad = contract_rows(group_in, low_grads)
    normed_grad = from_relative(
        head_scatter(low_grads, lambda rows: contract_cols(rows, project_all))
    )
    _, first_back = jax.vjp(norm_rows, inputs, norm_one)
    input_from, one_grad = first_back(normed_grad)
    input_grad = residual_grad + input_from
    depth = project.shape[0]
    project_part = wide_scatter(
        [project_grad[i * depth : (i + 1) * depth] for i in range(outer * inner)]
    )
    query_part = project_part[:, :query_width]
    keyvalue_part = jnp.stack(
        [project_part[:, query_width:value_from], project_part[:, value_from:gate_from]]
    )
    headgate_part = project_part[:, gate_from : gate_from + heads_local]
    output_part = wide_scatter(
        [output_grad[:, i * depth : (i + 1) * depth] for i in range(outer * inner)]
    )
    gain_partial = jnp.concatenate([one_grad, two_grad, query_gain_grad, key_gain_grad])
    parts = (query_part, keyvalue_part, headgate_part, output_part, expand_part, reduce_part)
    squares = jnp.zeros((), jnp.float32)
    for part_grad in parts:
        squares = squares + jnp.sum(part_grad * part_grad)
    totals = jnp.concatenate([gain_partial, squares[None]])
    for axis in ("c", "x", "b", "a"):
        totals = all_sum(totals, axis)
    gains_grad, square_total = totals[:-1], totals[-1]
    grad_norm = jnp.sqrt(square_total + jnp.sum(gains_grad * gains_grad))
    clip = CLIP_NORM / jnp.maximum(grad_norm, CLIP_NORM)
    gains_new = adam_step(gains, gains_grad * clip, gain_first, gain_second, GAIN_RATE, 0.0)
    masters = (
        query_weight,
        keyvalue_weight,
        headgate_weight,
        output_weight,
        expand_weight,
        reduce_weight,
    )
    states = (
        (query_first, query_second),
        (keyvalue_first, keyvalue_second),
        (headgate_first, headgate_second),
        (output_first, output_second),
        (expand_first, expand_second),
        (reduce_first, reduce_second),
    )
    results = [grad_norm, block_output, input_grad, gains_new[0], gains_new[1], gains_new[2]]
    for index in range(6):
        rate = OUTPUT_RATE if index == 3 else WEIGHT_RATE
        updated, first_new, second_new = adam_step(
            masters[index],
            parts[index] * clip,
            states[index][0],
            states[index][1],
            rate,
            WEIGHT_DECAY,
        )
        results = results + [updated, first_new, second_new, updated.astype(jnp.bfloat16)]
    return tuple(results)


def solution(mesh):
    heads, wides = mesh.shape["head"], mesh.shape["wide"]
    outer = 4 if wides % 4 == 0 else wides
    grid = Mesh(
        mesh.devices.reshape(heads // 2, 2, outer, wides // outer), ("x", "c", "a", "b")
    )
    wide, head = ("a", "b"), ("x", "c")
    rows = P(wide + head, None)
    by_wide = P(wide, head)
    stacked = P(None, wide, head)
    by_head = P(head, wide)
    widened = P(None, head, wide)
    return jax.shard_map(
        body,
        mesh=grid,
        in_specs=(rows, rows, P(wide), P(wide + head))
        + (P(),) * 4
        + (by_wide,) * 3
        + (stacked,) * 3
        + (by_wide,) * 3
        + (by_head,) * 3
        + (widened,) * 3
        + (by_wide,) * 3,
        out_specs=(P(), rows, rows)
        + (P(),) * 3
        + (by_wide,) * 4
        + (stacked,) * 4
        + (by_wide,) * 4
        + (by_head,) * 4
        + (widened,) * 4
        + (by_wide,) * 4,
        check_vma=False,
    )
```

```python
import functools

import jax
import jax.numpy as jnp
from jax import lax
from jax.experimental import pallas as pl
from jax.experimental.layout import Layout, with_layout_constraint
from jax.experimental.pallas import tpu as pltpu
from jax.sharding import Mesh
from jax.sharding import PartitionSpec as P

D = 2048
H = 16
HD = 128
KVH = 8
NDOM = 8
STEP = 10


NORM_EPS = 1e-06
ROPE_BASE = 1000000.0
MASK_FILL = -1e30
CLIP_NORM = 1.0
WEIGHT_RATE = 0.02
OUTPUT_RATE = 0.12
GAIN_RATE = 0.7
BETA_FIRST = 0.9
BETA_SECOND = 0.95
ADAM_EPS = 1e-08
WEIGHT_DECAY = 0.1
LOG2E = 1.4426950408889634


def rms_scale(values):
    return values * lax.rsqrt(jnp.mean(values * values, -1, keepdims=True) + NORM_EPS)


def norm_rows(values, gain):
    return rms_scale(values) * gain


def positions(segments):
    length = segments.shape[0]
    places = jnp.arange(length, dtype=jnp.int32)
    starts = jnp.concatenate([jnp.ones((1,), dtype=bool), segments[1:] != segments[:-1]])
    return places - lax.cummax(jnp.where(starts, places, 0), axis=0)


def contract_rows(left, right):
    return lax.dot_general(
        left, right, (((0,), (0,)), ((), ())), preferred_element_type=jnp.float32
    )


def contract_cols(left, right):
    return lax.dot_general(
        left, right, (((1,), (1,)), ((), ())), preferred_element_type=jnp.float32
    )


def swiglu_back(activation_grad, gate_pre, up_pre):
    gate_sigmoid = jax.nn.sigmoid(gate_pre)
    gate_grad = (
        activation_grad * up_pre * gate_sigmoid * (1.0 + gate_pre * (1.0 - gate_sigmoid))
    ).astype(jnp.bfloat16)
    up_grad = (activation_grad * gate_pre * gate_sigmoid).astype(jnp.bfloat16)
    return (gate_grad, up_grad)


def adam_step(weight, grad, first, second, rate, decay):
    first_new = BETA_FIRST * first + (1.0 - BETA_FIRST) * grad
    second_new = BETA_SECOND * second + (1.0 - BETA_SECOND) * grad * grad
    first_hat = first_new / (1.0 - BETA_FIRST**STEP)
    second_hat = second_new / (1.0 - BETA_SECOND**STEP)
    updated = weight - rate * (first_hat / (jnp.sqrt(second_hat) + ADAM_EPS) + decay * weight)
    return (updated, first_new, second_new)


def turn(values, cosine, sine):
    return values * cosine + pltpu.roll(values, HD // 2, 1) * sine


def dot_cols(left, right):
    return lax.dot_general(
        left, right, (((1,), (1,)), ((), ())), preferred_element_type=jnp.float32
    )


def dot_rows(left, right):
    return lax.dot_general(
        left, right, (((0,), (0,)), ((), ())), preferred_element_type=jnp.float32
    )


def allowed_keys(start, first, block, length, repeat):
    keys = lax.broadcasted_iota(jnp.int32, (block, length), 1)
    queries = first + lax.broadcasted_iota(jnp.int32, (block, length), 0)
    allowed = (keys >= start) & (keys <= queries)
    return jnp.concatenate([allowed] * repeat, 0)


def attend_kernel(
    heads,
    groups,
    block,
    slots,
    raw,
    start,
    cosine,
    sine,
    gain,
    query,
    key,
    value,
    attended,
    total_log,
    gated,
    gated_near,
):
    length = raw.shape[0]
    repeat = heads // groups
    key_from, value_from, gate_from = heads * HD, (heads + groups) * HD, (heads + 2 * groups) * HD
    cos, sin = cosine[...], sine[...]

    def prepared(column, gain_row):
        part = raw[:, column : column + HD]
        scale = lax.rsqrt(jnp.mean(part * part, -1, keepdims=True) + NORM_EPS)
        return turn(part * scale * gain_row, cos, sin).astype(jnp.bfloat16)

    for g in range(groups):
        key[:, g * HD : (g + 1) * HD] = prepared(key_from + g * HD, gain[1:2, :])
        value[:, g * HD : (g + 1) * HD] = raw[
            :, value_from + g * HD : value_from + (g + 1) * HD
        ].astype(jnp.bfloat16)
    for h in range(heads):
        query[:, h * HD : (h + 1) * HD] = prepared(h * HD, gain[0:1, :])
    total_log[...] = jnp.zeros(total_log.shape, jnp.float32)
    for i in range(length // block):
        rows = slice(i * block, (i + 1) * block)
        near = pl.ds(pl.multiple_of(slots[i] * block, block), block)
        seen = (i + 1) * block
        mask = allowed_keys(start[rows, :], i * block, block, seen, repeat)
        for g in range(groups):
            columns = slice(g * HD, (g + 1) * HD)
            hs = range(g * repeat, (g + 1) * repeat)
            queries = jnp.concatenate([query[rows, h * HD : (h + 1) * HD] for h in hs], 0)
            scores = dot_cols(queries, key[:seen, columns]) * (HD**-0.5 * LOG2E)
            scores = jnp.where(mask, scores, MASK_FILL)
            largest = jnp.max(scores, -1, keepdims=True)
            exponent = jnp.exp2(scores - largest)
            total = jnp.sum(exponent, -1, keepdims=True)
            result = jnp.dot(
                exponent.astype(jnp.bfloat16), value[:seen, columns], preferred_element_type=jnp.float32
            ) / total
            logs = largest + jnp.log2(total)
            for r, h in enumerate(hs):
                part = result[r * block : (r + 1) * block, :]
                gate = jax.nn.sigmoid(raw[rows, gate_from + h : gate_from + h + 1])
                attended[rows, h * HD : (h + 1) * HD] = part
                part_low = (part * gate).astype(jnp.bfloat16)
                gated[rows, h * HD : (h + 1) * HD] = part_low
                gated_near[near, h * HD : (h + 1) * HD] = part_low
                total_log[rows, h : h + 1] = logs[r * block : (r + 1) * block, :]


def in_vmem(count):
    return [pl.BlockSpec(memory_space=pltpu.SMEM)] + [pl.BlockSpec(memory_space=pltpu.VMEM)] * count


def attend(slots, raw, start, cosine, sine, gain, heads, groups):
    length = raw.shape[0]
    low = jnp.bfloat16
    return pl.pallas_call(
        functools.partial(attend_kernel, heads, groups, length // slots.shape[0]),
        in_specs=in_vmem(5),
        out_shape=(
            jax.ShapeDtypeStruct((length, heads * HD), low),
            jax.ShapeDtypeStruct((length, groups * HD), low),
            jax.ShapeDtypeStruct((length, groups * HD), low),
            jax.ShapeDtypeStruct((length, heads * HD), jnp.float32),
            jax.ShapeDtypeStruct((length, HD), jnp.float32),
            jax.ShapeDtypeStruct((length, heads * HD), low),
            jax.ShapeDtypeStruct((length, heads * HD), low),
        ),
        compiler_params=pltpu.CompilerParams(vmem_limit_bytes=56 * 2**20),
        cost_estimate=pl.CostEstimate(
            flops=4 * heads * length * length * HD,
            bytes_accessed=raw.size * 4 + length * heads * HD * 10,
            transcendentals=heads * length * length,
        ),
    )(slots, raw, start, cosine, sine, gain)


def attend_back_kernel(
    heads,
    groups,
    block,
    slots,
    gated_grad,
    raw,
    start,
    cosine,
    sine,
    gain,
    query,
    key,
    value,
    attended,
    total_log,
    grads,
    grads_near,
    gain_grads,
    low_grad,
    delta,
    query_sum,
    key_sum,
    value_sum,
):
    length = raw.shape[0]
    repeat = heads // groups
    key_from, value_from, gate_from = heads * HD, (heads + groups) * HD, (heads + 2 * groups) * HD
    cos, sin = cosine[...], sine[...]
    scale = HD**-0.5
    nears = [
        pl.ds(pl.multiple_of(slots[i] * block, block), block) for i in range(length // block)
    ]

    def unprepared(grad, column, gain_row):
        part = raw[:, column : column + HD]
        inverse = lax.rsqrt(jnp.mean(part * part, -1, keepdims=True) + NORM_EPS)
        unit = part * inverse
        back = grad * cos - pltpu.roll(grad, HD // 2, 1) * sin
        inner = back * gain_row
        mean = jnp.mean(inner * unit, -1, keepdims=True)
        result = inverse * (inner - unit * mean)
        return result.astype(jnp.bfloat16), jnp.sum(back * unit, 0, keepdims=True)

    grads[:, gate_from:] = jnp.zeros((length, grads.shape[1] - gate_from), jnp.bfloat16)
    for h in range(heads):
        columns = slice(h * HD, (h + 1) * HD)
        gate = jax.nn.sigmoid(raw[:, gate_from + h : gate_from + h + 1])
        outer = jnp.concatenate([gated_grad[near, columns] for near in nears], 0)
        result = attended[:, columns]
        low = (outer * gate).astype(jnp.bfloat16)
        low_grad[:, columns] = low
        logit = jnp.sum(outer * result, -1, keepdims=True) * gate * (1.0 - gate)
        grads[:, gate_from + h : gate_from + h + 1] = logit.astype(jnp.bfloat16)
        delta[:, h : h + 1] = jnp.sum(low.astype(jnp.float32) * result, -1, keepdims=True)
    key_sum[...] = jnp.zeros(key_sum.shape, jnp.float32)
    value_sum[...] = jnp.zeros(value_sum.shape, jnp.float32)
    for i in range(length // block):
        rows = slice(i * block, (i + 1) * block)
        seen = (i + 1) * block
        mask = allowed_keys(start[rows, :], i * block, block, seen, repeat)
        for g in range(groups):
            columns = slice(g * HD, (g + 1) * HD)
            hs = range(g * repeat, (g + 1) * repeat)
            queries = jnp.concatenate([query[rows, h * HD : (h + 1) * HD] for h in hs], 0)
            outers = jnp.concatenate([low_grad[rows, h * HD : (h + 1) * HD] for h in hs], 0)
            logs = jnp.concatenate([total_log[rows, h : h + 1] for h in hs], 0)
            deltas = jnp.concatenate([delta[rows, h : h + 1] for h in hs], 0)
            keys, values = key[:seen, columns], value[:seen, columns]
            scores = dot_cols(queries, keys) * (scale * LOG2E)
            probs = jnp.exp2(jnp.where(mask, scores - logs, MASK_FILL))
            prob_grad = dot_cols(outers, values)
            score_grad = (probs * (prob_grad - deltas)).astype(jnp.bfloat16)
            moved = jnp.dot(score_grad, keys, preferred_element_type=jnp.float32) * scale
            for r, h in enumerate(hs):
                query_sum[rows, h * HD : (h + 1) * HD] = moved[r * block : (r + 1) * block, :]
            key_sum[:seen, columns] += dot_rows(score_grad, queries)
            value_sum[:seen, columns] += dot_rows(probs.astype(jnp.bfloat16), outers)
    gain_grads[...] = jnp.zeros(gain_grads.shape, jnp.float32)
    for h in range(heads):
        part, gain_part = unprepared(query_sum[:, h * HD : (h + 1) * HD], h * HD, gain[0:1, :])
        grads[:, h * HD : (h + 1) * HD] = part
        gain_grads[0:1, :] += gain_part
    for g in range(groups):
        columns = slice(g * HD, (g + 1) * HD)
        part, gain_part = unprepared(
            key_sum[:, columns] * scale, key_from + g * HD, gain[1:2, :]
        )
        grads[:, key_from + g * HD : key_from + (g + 1) * HD] = part
        gain_grads[1:2, :] += gain_part
        grads[:, value_from + g * HD : value_from + (g + 1) * HD] = value_sum[:, columns].astype(
            jnp.bfloat16
        )
    for i, near in enumerate(nears):
        grads_near[near, :] = grads[i * block : (i + 1) * block, :]


def attend_back(slots, gated_grad, raw, start, cosine, sine, gain, saved, heads, groups):
    length = raw.shape[0]
    query, key, value, attended, total_log = saved
    return pl.pallas_call(
        functools.partial(attend_back_kernel, heads, groups, length // slots.shape[0]),
        in_specs=in_vmem(11),
        out_shape=(
            jax.ShapeDtypeStruct(raw.shape, jnp.bfloat16),
            jax.ShapeDtypeStruct(raw.shape, jnp.bfloat16),
            jax.ShapeDtypeStruct((2, HD), jnp.float32),
        ),
        scratch_shapes=[
            pltpu.VMEM((length, heads * HD), jnp.bfloat16),
            pltpu.VMEM((length, HD), jnp.float32),
            pltpu.VMEM((length, heads * HD), jnp.float32),
            pltpu.VMEM((length, groups * HD), jnp.float32),
            pltpu.VMEM((length, groups * HD), jnp.float32),
        ],
        compiler_params=pltpu.CompilerParams(vmem_limit_bytes=56 * 2**20),
        cost_estimate=pl.CostEstimate(
            flops=10 * heads * length * length * HD,
            bytes_accessed=raw.size * 6 + length * heads * HD * 12,
            transcendentals=heads * length * length,
        ),
    )(slots, gated_grad, raw, start, cosine, sine, gain, query, key, value, attended, total_log)


def rope_tables(places):
    half = HD // 2
    freqs = ROPE_BASE ** (-2.0 * jnp.arange(half, dtype=jnp.float32) / HD)
    angles = places.astype(jnp.float32)[:, None] * freqs[None, :]
    cosine, sine = jnp.cos(angles), jnp.sin(angles)
    return jnp.concatenate([cosine, cosine], 1), jnp.concatenate([-sine, sine], 1)


def tie(*values):
    return lax.optimization_barrier(values)


TEAM = 4


def swapped(value, axis, flip):
    size = lax.axis_size(axis)
    return lax.ppermute(value, axis, [(i, i ^ flip) for i in range(size)])


def hop(value, axis):
    size = lax.axis_size(axis)
    return lax.ppermute(value, axis, [(i, (i - 1) % size) for i in range(size)])


def ring_gather(value, axis):
    pieces = [value]
    for _ in range(lax.axis_size(axis) - 1):
        pieces.append(hop(pieces[-1], axis))
    return pieces


def ring_scatter(parts, axis):
    size = lax.axis_size(axis)
    total = parts[1 % size]
    for step in range(1, size):
        total = parts[(step + 1) % size] + hop(total.astype(jnp.bfloat16), axis).astype(jnp.float32)
    return total


def wide_shape():
    size = lax.axis_size("w")
    return TEAM, size // TEAM


def wide_from(value, outer_step, inner_step):
    outer, inner = wide_shape()
    pairs = []
    for a in range(outer):
        for b in range(inner):
            source = (a + outer_step) % outer * inner + (b + inner_step) % inner
            pairs.append((source, a * inner + b))
    return lax.ppermute(value, "w", pairs)


def inner_gather(value):
    pieces = [value]
    for _ in range(wide_shape()[1] - 1):
        pieces.append(wide_from(pieces[-1], 0, 1))
    return pieces


def inner_scatter(parts):
    size = wide_shape()[1]
    total = parts[1 % size]
    for step in range(1, size):
        moved = wide_from(total.astype(jnp.bfloat16), 0, 1)
        total = parts[(step + 1) % size] + moved.astype(jnp.float32)
    return total


def wide_slots():
    outer, inner = wide_shape()
    me = lax.axis_index("w")
    a_me, b_me = me // inner, lax.rem(me, inner)
    return [
        [lax.rem(a_me + i, outer) * inner + lax.rem(b_me + j, inner) for j in range(inner)]
        for i in range(outer)
    ]


def outer_shift(value, step):
    return wide_from(value, step, 0)


def all_sum(value, axis):
    size = lax.axis_size(axis)
    if size & (size - 1):
        return lax.psum(value, axis)
    step = 1
    while step < size:
        value = value + swapped(value, axis, step)
        step = 2 * step
    return value


def assemble(pieces, axis):
    first = pieces[0][0]
    size = first.shape[axis]
    shape = list(first.shape)
    shape[axis] = size * len(pieces) * len(pieces[0])
    result = jnp.zeros(shape, first.dtype)
    for row, slots in zip(pieces, wide_slots()):
        for piece, slot in zip(row, slots):
            result = lax.dynamic_update_slice_in_dim(result, piece, slot * size, axis)
    return result


def near_slots():
    x_size = lax.axis_size("x")
    x_me, c_me = lax.axis_index("x"), lax.axis_index("c")
    return jnp.stack(
        [
            (core ^ c_me) * x_size + lax.rem(x + x_size - x_me, x_size)
            for x in range(x_size)
            for core in range(2)
        ]
    ).astype(jnp.int32)


def pinned(values):
    return with_layout_constraint(values, Layout(tuple(range(values.ndim))))


def by_x(total):
    x_size = lax.axis_size("x")
    rows = total.shape[0] // x_size
    return [total[i * rows : (i + 1) * rows] for i in range(x_size)]


def body(
    tokens,
    cotangent,
    segment_ids,
    domain_ids,
    domain_weights,
    gains,
    gain_first,
    gain_second,
    query_weight,
    query_first,
    query_second,
    keyvalue_weight,
    keyvalue_first,
    keyvalue_second,
    headgate_weight,
    headgate_first,
    headgate_second,
    output_weight,
    output_first,
    output_second,
    expand_weight,
    expand_first,
    expand_second,
    reduce_weight,
    reduce_first,
    reduce_second,
):
    head_devices = lax.axis_size("x") * lax.axis_size("c")
    core = lax.axis_index("c")
    outer, inner = wide_shape()
    heads = H // head_devices
    groups = KVH // head_devices
    low = jnp.bfloat16
    wide = jnp.float32
    labels = jnp.arange(NDOM, dtype=jnp.int32)
    onehot = domain_ids[:, None] == labels[None, :]
    token_weight = jnp.sum(jnp.where(onehot, domain_weights[None, :], 0.0), -1)
    upstream = cotangent.astype(wide) * token_weight[:, None]
    norm_one = gains[:D]
    norm_two = gains[D : 2 * D]
    head_gains = gains[2 * D :].reshape(2, HD)
    inputs = tokens.astype(wide)
    normed = norm_rows(inputs, norm_one).astype(low)
    depth = query_weight.shape[0]
    query_width, key_width = query_weight.shape[1], keyvalue_weight.shape[2]
    value_from = query_width + key_width
    gate_from = value_from + key_width
    project = jnp.concatenate(
        [
            query_weight,
            keyvalue_weight[0],
            keyvalue_weight[1],
            headgate_weight,
            jnp.zeros((depth, -heads % 128), wide),
        ],
        1,
    ).astype(low)
    group_in = lax.all_gather(normed, ("x", "c"), axis=0, tiled=True)
    output_low = output_weight.astype(low)
    upstream_low = upstream.astype(low)
    expand_low = jnp.concatenate([expand_weight[0], expand_weight[1]], 1).astype(low)
    reduce_low = reduce_weight.astype(low)
    hidden = reduce_low.shape[0]

    def expand_whole(piece):
        return lax.all_gather(piece, ("x", "c"), axis=0, tiled=True)

    def reduce_whole(piece):
        return lax.all_gather(piece, ("x", "c"), axis=1, tiled=True)

    expand_all = [expand_whole(expand_low)]
    reduce_all = [reduce_whole(reduce_low)]

    group_size = group_in.shape[0]
    places = positions(segment_ids)
    starts = (jnp.arange(group_size, dtype=jnp.int32) - places)[:, None]
    cosine, sine = rope_tables(places)

    near = near_slots()
    x_size = lax.axis_size("x")

    row = project
    project_pieces = []
    for _ in range(outer - 1):
        moved, across, starts, cosine, sine = tie(
            wide_from(row, 1, 0), inner_gather(row), starts, cosine, sine
        )
        project_pieces.append(across)
        row = moved
    row, output_low, upstream_low = tie(row, output_low, upstream_low)
    output_rows = [output_low] + [wide_from(output_low, i, 0) for i in range(1, outer)]
    sides = [expand_low[:, :hidden], expand_low[:, hidden:]]
    across, output_rows, upstream_low, sides = tie(
        inner_gather(row), output_rows, upstream_low, sides
    )
    project_pieces.append(across)
    output_pieces = [inner_gather(piece) for piece in output_rows]
    upstream_parts = [upstream_low, outer_shift(upstream_low, 1)]
    project_all = assemble(project_pieces, 0)
    raw = jnp.dot(group_in, project_all, preferred_element_type=wide)
    raw, output_pieces, upstream_parts, sides = tie(raw, output_pieces, upstream_parts, sides)
    gate_pieces = inner_gather(sides[0])
    upstream_parts.append(outer_shift(upstream_parts[-1], 1))
    output_all = assemble(output_pieces, 1)
    kept = attend(near, raw, starts, cosine, sine, head_gains, heads, groups)
    kept, output_all, upstream_parts, gate_pieces, sides = tie(
        kept, output_all, upstream_parts, gate_pieces, sides
    )
    up_pieces = inner_gather(sides[1])
    upstream_parts.append(outer_shift(upstream_parts[-1], 1))
    query, key, value, attended, total_log, gated, gated_near = kept
    half = gated.shape[0] // 2

    def projected(rows):
        return jnp.dot(rows, output_all, preferred_element_type=wide)

    received = swapped(projected(gated_near[half:]).astype(low), "c", 1)
    attention = projected(gated_near[:half]) + received.astype(wide)
    attention = by_x(attention)
    split = attention[0].shape[0] // 2
    first = ring_scatter([part[:split] for part in attention], "x")
    second = ring_scatter([part[split:] for part in attention], "x")
    first, up_pieces, reduce_low, upstream_parts = tie(
        first, up_pieces, reduce_low, upstream_parts
    )
    expand_all = expand_all + [
        expand_whole(jnp.concatenate(pair, 1)) for pair in zip(gate_pieces[1:], up_pieces[1:])
    ]
    reduce_pieces = inner_gather(reduce_low)
    attention = jnp.concatenate([first, second], 0)
    residual = inputs + attention
    mixed = norm_rows(residual, norm_two).astype(low)

    def hidden_part(k, j):
        both = jnp.dot(mixed_parts[k], expand_all[j], preferred_element_type=wide)
        gate_pre, up_pre = both[:, :hidden], both[:, hidden:]
        activation = (jax.nn.silu(gate_pre) * up_pre).astype(low)
        activation_grad = contract_cols(upstream_parts[k], reduce_all[j])
        return activation, jnp.concatenate(swiglu_back(activation_grad, gate_pre, up_pre), 1)

    def mixed_back(parts, j):
        return contract_cols(parts[1], expand_all[j])

    def lowered(parts, j):
        return jnp.dot(parts[0], reduce_all[j], preferred_element_type=wide)

    done = {}
    grad_sums = {}
    output_sums = {}

    def begin(k):
        done[k, 0] = hidden_part(k, 0)
        grad_sums[k] = mixed_back(done[k, 0], 0)
        output_sums[k] = lowered(done[k, 0], 0)

    def rest(k):
        for j in range(1, inner):
            done[k, j] = hidden_part(k, j)
            grad_sums[k] = grad_sums[k] + mixed_back(done[k, j], j)

    def joined(which, j):
        return jnp.concatenate([done[k, j][which] for k in range(outer)], 0)

    def expand_back(j):
        return lax.psum_scatter(
            contract_rows(mixed_all, joined(1, j)).astype(low),
            ("x", "c"),
            scatter_dimension=0,
            tiled=True,
        )

    def reduce_back(j):
        return lax.psum_scatter(
            contract_rows(joined(0, j), upstream_all).astype(low),
            ("x", "c"),
            scatter_dimension=1,
            tiled=True,
        )

    mixed_parts = [mixed]
    moved = outer_shift(mixed, 1)
    begin(0)
    moved, done, grad_sums, output_sums, reduce_pieces = tie(
        moved, done, grad_sums, output_sums, reduce_pieces
    )
    reduce_all = reduce_all + [reduce_whole(piece) for piece in reduce_pieces[1:]]
    mixed_parts.append(moved)
    moved = outer_shift(moved, 1)
    begin(1)
    moved, done, grad_sums, output_sums = tie(moved, done, grad_sums, output_sums)
    mixed_parts.append(moved)
    moved = outer_shift(moved, 1)
    begin(2)
    rest(1)
    moved, done, grad_sums, output_sums = tie(moved, done, grad_sums, output_sums)
    mixed_parts.append(moved)
    moved = outer_shift(grad_sums[1].astype(low), 1)
    rest(2)
    begin(3)
    moved, done, grad_sums, output_sums = tie(moved, done, grad_sums, output_sums)
    moved = outer_shift((grad_sums[2] + moved.astype(wide)).astype(low), 1)
    rest(3)
    rest(0)
    mixed_all = jnp.concatenate(mixed_parts, 0)
    upstream_all = jnp.concatenate(upstream_parts, 0)
    moved, done, grad_sums, output_sums, mixed_all, upstream_all = tie(
        moved, done, grad_sums, output_sums, mixed_all, upstream_all
    )
    sent = (grad_sums[3] + moved.astype(wide)).astype(low)
    early, late = outer_shift(sent[:split], 1), outer_shift(sent[split:], 1)
    for k in range(outer):
        for j in range(1, inner):
            output_sums[k] = output_sums[k] + lowered(done[k, j], j)
    early, done, upstream_all, mixed_all = tie(early, done, upstream_all, mixed_all)
    expand_wide = [None] * inner
    reduce_wide = [None] * inner
    for j in range(1, inner):
        expand_wide[j] = expand_back(j)
    late, done, upstream_all, mixed_all = tie(late, done, upstream_all, mixed_all)
    moved = jnp.concatenate([early, late], 0)
    mixed_grad = grad_sums[0] + moved.astype(wide)
    _, second_back = jax.vjp(norm_rows, residual, norm_two)
    residual_from, two_grad = second_back(mixed_grad)
    residual_grad = upstream + residual_from
    residual_low = residual_grad.astype(low)
    output_total = outer_shift(output_sums[1].astype(low), 1)
    early_row = ring_gather(residual_low[:split], "x")
    late_row = ring_gather(residual_low[split:], "x")
    early_row, done, upstream_all, mixed_all = tie(early_row, done, upstream_all, mixed_all)
    for j in range(1, inner):
        reduce_wide[j] = reduce_back(j)
    expand_wide[0] = expand_back(0)
    late_row, output_total, done, upstream_all = tie(late_row, output_total, done, upstream_all)
    residual_row = [jnp.concatenate(pair, 0) for pair in zip(early_row, late_row)]
    residual_all = jnp.concatenate(
        residual_row + [swapped(piece, "c", 1) for piece in residual_row], 0
    )
    slots = wide_slots()

    def wide_parts(whole, axis, i):
        return [lax.dynamic_slice_in_dim(whole, slot * depth, depth, axis) for slot in slots[i]]

    gated_grad = contract_cols(residual_all, output_all)
    output_total = outer_shift((output_sums[2] + output_total.astype(wide)).astype(low), 1)
    back = attend_back(
        near,
        gated_grad,
        raw,
        starts,
        cosine,
        sine,
        head_gains,
        (query, key, value, attended, total_log),
        heads,
        groups,
    )
    expand_both = inner_scatter([part.astype(wide) for part in expand_wide])
    back, output_total, expand_both, done, residual_all = tie(
        back, output_total, expand_both, done, residual_all
    )
    low_grads, low_near, head_gain_grads = back
    output_total = outer_shift((output_sums[3] + output_total.astype(wide)).astype(low), 1)
    project_grad = pinned(contract_rows(group_in, low_grads))
    project_wide = [None] * outer
    order = [(step + 1) % outer for step in range(outer)]
    project_wide[order[0]] = inner_scatter(wide_parts(project_grad, 0, order[0]))
    output_grad = contract_rows(gated_near, residual_all)

    def output_rows_of(i):
        return jnp.concatenate(wide_parts(output_grad, 1, i), 1)

    def normed_back(rows):
        return contract_cols(rows, project_all)

    received = swapped(normed_back(low_near[half:]).astype(low), "c", 1)
    normed_grad = normed_back(low_near[:half]) + received.astype(wide)
    normed_grad, project_wide[order[0]], project_grad, output_total = tie(
        normed_grad, project_wide[order[0]], project_grad, output_total
    )
    normed_grad = ring_scatter(by_x(normed_grad), "x")
    project_total = project_wide[order[0]]
    output_part = output_rows_of(order[0])
    for i in order[1:]:
        moved, output_new, across = tie(
            outer_shift(project_total.astype(low), 1),
            outer_shift(output_part.astype(low), 1),
            inner_scatter(wide_parts(project_grad, 0, i)),
        )
        project_total = across + moved.astype(wide)
        output_part = output_rows_of(i) + output_new.astype(wide)
    project_part = pinned(project_total)
    output_part = inner_scatter([output_part[:, j * depth : (j + 1) * depth] for j in range(inner)])
    reduce_wide[0] = reduce_back(0)
    block_output = (residual + output_sums[0] + output_total.astype(wide)).astype(low)
    _, first_back = jax.vjp(norm_rows, inputs, norm_one)
    input_from, one_grad = first_back(normed_grad)
    input_grad = residual_grad + input_from
    reduce_part = inner_scatter([part.astype(wide) for part in reduce_wide])
    expand_part = jnp.stack([expand_both[:, :hidden], expand_both[:, hidden:]])
    query_part = project_part[:, :query_width]
    keyvalue_part = jnp.stack(
        [project_part[:, query_width:value_from], project_part[:, value_from:gate_from]]
    )
    headgate_part = project_part[:, gate_from : gate_from + heads]
    gain_partial = jnp.concatenate([one_grad, two_grad, head_gain_grads.reshape(-1)])
    parts = (query_part, keyvalue_part, headgate_part, output_part, expand_part, reduce_part)
    squares = jnp.zeros((), jnp.float32)
    for part_grad in parts:
        squares = squares + jnp.sum(part_grad * part_grad)
    totals = jnp.concatenate([gain_partial, squares[None]])
    for axis in ("c", "x", "w"):
        totals = all_sum(totals, axis)
    gains_grad, square_total = totals[:-1], totals[-1]
    grad_norm = jnp.sqrt(square_total + jnp.sum(gains_grad * gains_grad))
    clip = CLIP_NORM / jnp.maximum(grad_norm, CLIP_NORM)
    gains_new = adam_step(gains, gains_grad * clip, gain_first, gain_second, GAIN_RATE, 0.0)
    masters = (
        query_weight,
        keyvalue_weight,
        headgate_weight,
        output_weight,
        expand_weight,
        reduce_weight,
    )
    states = (
        (query_first, query_second),
        (keyvalue_first, keyvalue_second),
        (headgate_first, headgate_second),
        (output_first, output_second),
        (expand_first, expand_second),
        (reduce_first, reduce_second),
    )
    results = [grad_norm, block_output, input_grad, gains_new[0], gains_new[1], gains_new[2]]
    for index in range(6):
        rate = OUTPUT_RATE if index == 3 else WEIGHT_RATE
        updated, first_new, second_new = adam_step(
            masters[index],
            parts[index] * clip,
            states[index][0],
            states[index][1],
            rate,
            WEIGHT_DECAY,
        )
        results = results + [updated, first_new, second_new, updated.astype(low)]
    return tuple(results)


def solution(mesh):
    heads, wides = mesh.shape["head"], mesh.shape["wide"]
    grid = Mesh(mesh.devices.reshape(heads // 2, 2, wides), ("x", "c", "w"))
    wide, head = ("w",), ("x", "c")
    rows = P(wide + head, None)
    by_wide = P(wide, head)
    stacked = P(None, wide, head)
    by_head = P(head, wide)
    widened = P(None, head, wide)
    return jax.shard_map(
        body,
        mesh=grid,
        in_specs=(rows, rows, P(wide), P(wide + head))
        + (P(),) * 4
        + (by_wide,) * 3
        + (stacked,) * 3
        + (by_wide,) * 3
        + (by_head,) * 3
        + (widened,) * 3
        + (by_wide,) * 3,
        out_specs=(P(), rows, rows)
        + (P(),) * 3
        + (by_wide,) * 4
        + (stacked,) * 4
        + (by_wide,) * 4
        + (by_head,) * 4
        + (widened,) * 4
        + (by_wide,) * 4,
        check_vma=False,
    )
```

```python
import functools

import jax
import jax.numpy as jnp
from jax import lax
from jax.experimental import pallas as pl
from jax.experimental.layout import Layout, with_layout_constraint
from jax.experimental.pallas import tpu as pltpu
from jax.sharding import Mesh
from jax.sharding import PartitionSpec as P

D = 2048
H = 16
HD = 128
KVH = 8
NDOM = 8
STEP = 10


NORM_EPS = 1e-06
ROPE_BASE = 1000000.0
MASK_FILL = -1e30
CLIP_NORM = 1.0
WEIGHT_RATE = 0.02
OUTPUT_RATE = 0.12
GAIN_RATE = 0.7
BETA_FIRST = 0.9
BETA_SECOND = 0.95
ADAM_EPS = 1e-08
WEIGHT_DECAY = 0.1
LOG2E = 1.4426950408889634


def rms_scale(values):
    return values * lax.rsqrt(jnp.mean(values * values, -1, keepdims=True) + NORM_EPS)


def norm_rows(values, gain):
    return rms_scale(values) * gain


def positions(segments):
    length = segments.shape[0]
    places = jnp.arange(length, dtype=jnp.int32)
    starts = jnp.concatenate([jnp.ones((1,), dtype=bool), segments[1:] != segments[:-1]])
    return places - lax.cummax(jnp.where(starts, places, 0), axis=0)


def contract_rows(left, right):
    return lax.dot_general(
        left, right, (((0,), (0,)), ((), ())), preferred_element_type=jnp.float32
    )


def contract_cols(left, right):
    return lax.dot_general(
        left, right, (((1,), (1,)), ((), ())), preferred_element_type=jnp.float32
    )


def swiglu_back(activation_grad, gate_pre, up_pre):
    gate_sigmoid = jax.nn.sigmoid(gate_pre)
    gate_grad = (
        activation_grad * up_pre * gate_sigmoid * (1.0 + gate_pre * (1.0 - gate_sigmoid))
    ).astype(jnp.bfloat16)
    up_grad = (activation_grad * gate_pre * gate_sigmoid).astype(jnp.bfloat16)
    return (gate_grad, up_grad)


def adam_step(weight, grad, first, second, rate, decay):
    first_new = BETA_FIRST * first + (1.0 - BETA_FIRST) * grad
    second_new = BETA_SECOND * second + (1.0 - BETA_SECOND) * grad * grad
    first_hat = first_new / (1.0 - BETA_FIRST**STEP)
    second_hat = second_new / (1.0 - BETA_SECOND**STEP)
    updated = weight - rate * (first_hat / (jnp.sqrt(second_hat) + ADAM_EPS) + decay * weight)
    return (updated, first_new, second_new)


def turn(values, cosine, sine):
    return values * cosine + pltpu.roll(values, HD // 2, 1) * sine


def dot_cols(left, right):
    return lax.dot_general(
        left, right, (((1,), (1,)), ((), ())), preferred_element_type=jnp.float32
    )


def dot_rows(left, right):
    return lax.dot_general(
        left, right, (((0,), (0,)), ((), ())), preferred_element_type=jnp.float32
    )


def allowed_keys(start, first, block, length, repeat):
    keys = lax.broadcasted_iota(jnp.int32, (block, length), 1)
    queries = first + lax.broadcasted_iota(jnp.int32, (block, length), 0)
    allowed = (keys >= start) & (keys <= queries)
    return jnp.concatenate([allowed] * repeat, 0)


def attend_kernel(
    heads,
    groups,
    block,
    slots,
    raw,
    start,
    cosine,
    sine,
    gain,
    query,
    key,
    value,
    attended,
    total_log,
    gated,
    gated_near,
):
    length = raw.shape[0]
    repeat = heads // groups
    key_from, value_from, gate_from = heads * HD, (heads + groups) * HD, (heads + 2 * groups) * HD
    cos, sin = cosine[...], sine[...]

    def prepared(column, gain_row):
        part = raw[:, column : column + HD]
        scale = lax.rsqrt(jnp.mean(part * part, -1, keepdims=True) + NORM_EPS)
        return turn(part * scale * gain_row, cos, sin).astype(jnp.bfloat16)

    for g in range(groups):
        key[:, g * HD : (g + 1) * HD] = prepared(key_from + g * HD, gain[1:2, :])
        value[:, g * HD : (g + 1) * HD] = raw[
            :, value_from + g * HD : value_from + (g + 1) * HD
        ].astype(jnp.bfloat16)
    for h in range(heads):
        query[:, h * HD : (h + 1) * HD] = prepared(h * HD, gain[0:1, :])
    total_log[...] = jnp.zeros(total_log.shape, jnp.float32)
    for i in range(length // block):
        rows = slice(i * block, (i + 1) * block)
        near = pl.ds(pl.multiple_of(slots[i] * block, block), block)
        seen = (i + 1) * block
        mask = allowed_keys(start[rows, :], i * block, block, seen, repeat)
        for g in range(groups):
            columns = slice(g * HD, (g + 1) * HD)
            hs = range(g * repeat, (g + 1) * repeat)
            queries = jnp.concatenate([query[rows, h * HD : (h + 1) * HD] for h in hs], 0)
            scores = dot_cols(queries, key[:seen, columns]) * (HD**-0.5 * LOG2E)
            exponent = jnp.exp2(jnp.where(mask, scores, MASK_FILL))
            total = jnp.sum(exponent, -1, keepdims=True)
            result = jnp.dot(
                exponent.astype(jnp.bfloat16), value[:seen, columns], preferred_element_type=jnp.float32
            ) / total
            logs = jnp.log2(total)
            for r, h in enumerate(hs):
                part = result[r * block : (r + 1) * block, :]
                gate = jax.nn.sigmoid(raw[rows, gate_from + h : gate_from + h + 1])
                attended[rows, h * HD : (h + 1) * HD] = part
                part_low = (part * gate).astype(jnp.bfloat16)
                gated[rows, h * HD : (h + 1) * HD] = part_low
                gated_near[near, h * HD : (h + 1) * HD] = part_low
                total_log[rows, h : h + 1] = logs[r * block : (r + 1) * block, :]


def in_vmem(count):
    return [pl.BlockSpec(memory_space=pltpu.SMEM)] + [pl.BlockSpec(memory_space=pltpu.VMEM)] * count


def attend(slots, raw, start, cosine, sine, gain, heads, groups):
    length = raw.shape[0]
    low = jnp.bfloat16
    return pl.pallas_call(
        functools.partial(attend_kernel, heads, groups, length // slots.shape[0]),
        in_specs=in_vmem(5),
        out_shape=(
            jax.ShapeDtypeStruct((length, heads * HD), low),
            jax.ShapeDtypeStruct((length, groups * HD), low),
            jax.ShapeDtypeStruct((length, groups * HD), low),
            jax.ShapeDtypeStruct((length, heads * HD), jnp.float32),
            jax.ShapeDtypeStruct((length, HD), jnp.float32),
            jax.ShapeDtypeStruct((length, heads * HD), low),
            jax.ShapeDtypeStruct((length, heads * HD), low),
        ),
        compiler_params=pltpu.CompilerParams(vmem_limit_bytes=56 * 2**20),
        cost_estimate=pl.CostEstimate(
            flops=4 * heads * length * length * HD,
            bytes_accessed=raw.size * 4 + length * heads * HD * 10,
            transcendentals=heads * length * length,
        ),
    )(slots, raw, start, cosine, sine, gain)


def attend_back_kernel(
    heads,
    groups,
    block,
    slots,
    gated_grad,
    raw,
    start,
    cosine,
    sine,
    gain,
    query,
    key,
    value,
    attended,
    total_log,
    grads,
    grads_near,
    gain_grads,
    low_grad,
    delta,
    query_sum,
    key_sum,
    value_sum,
):
    length = raw.shape[0]
    repeat = heads // groups
    key_from, value_from, gate_from = heads * HD, (heads + groups) * HD, (heads + 2 * groups) * HD
    cos, sin = cosine[...], sine[...]
    scale = HD**-0.5
    nears = [
        pl.ds(pl.multiple_of(slots[i] * block, block), block) for i in range(length // block)
    ]

    def unprepared(grad, column, gain_row):
        part = raw[:, column : column + HD]
        inverse = lax.rsqrt(jnp.mean(part * part, -1, keepdims=True) + NORM_EPS)
        unit = part * inverse
        back = grad * cos - pltpu.roll(grad, HD // 2, 1) * sin
        inner = back * gain_row
        mean = jnp.mean(inner * unit, -1, keepdims=True)
        result = inverse * (inner - unit * mean)
        return result.astype(jnp.bfloat16), jnp.sum(back * unit, 0, keepdims=True)

    grads[:, gate_from:] = jnp.zeros((length, grads.shape[1] - gate_from), jnp.bfloat16)
    for h in range(heads):
        columns = slice(h * HD, (h + 1) * HD)
        gate = jax.nn.sigmoid(raw[:, gate_from + h : gate_from + h + 1])
        outer = jnp.concatenate([gated_grad[near, columns] for near in nears], 0)
        result = attended[:, columns]
        low = (outer * gate).astype(jnp.bfloat16)
        low_grad[:, columns] = low
        logit = jnp.sum(outer * result, -1, keepdims=True) * gate * (1.0 - gate)
        grads[:, gate_from + h : gate_from + h + 1] = logit.astype(jnp.bfloat16)
        delta[:, h : h + 1] = jnp.sum(low.astype(jnp.float32) * result, -1, keepdims=True)
    key_sum[...] = jnp.zeros(key_sum.shape, jnp.float32)
    value_sum[...] = jnp.zeros(value_sum.shape, jnp.float32)
    for i in range(length // block):
        rows = slice(i * block, (i + 1) * block)
        seen = (i + 1) * block
        mask = allowed_keys(start[rows, :], i * block, block, seen, repeat)
        for g in range(groups):
            columns = slice(g * HD, (g + 1) * HD)
            hs = range(g * repeat, (g + 1) * repeat)
            queries = jnp.concatenate([query[rows, h * HD : (h + 1) * HD] for h in hs], 0)
            outers = jnp.concatenate([low_grad[rows, h * HD : (h + 1) * HD] for h in hs], 0)
            logs = jnp.concatenate([total_log[rows, h : h + 1] for h in hs], 0)
            deltas = jnp.concatenate([delta[rows, h : h + 1] for h in hs], 0)
            keys, values = key[:seen, columns], value[:seen, columns]
            scores = dot_cols(queries, keys) * (scale * LOG2E)
            probs = jnp.exp2(jnp.where(mask, scores - logs, MASK_FILL))
            prob_grad = dot_cols(outers, values)
            score_grad = (probs * (prob_grad - deltas)).astype(jnp.bfloat16)
            moved = jnp.dot(score_grad, keys, preferred_element_type=jnp.float32) * scale
            for r, h in enumerate(hs):
                query_sum[rows, h * HD : (h + 1) * HD] = moved[r * block : (r + 1) * block, :]
            key_sum[:seen, columns] += dot_rows(score_grad, queries)
            value_sum[:seen, columns] += dot_rows(probs.astype(jnp.bfloat16), outers)
    gain_grads[...] = jnp.zeros(gain_grads.shape, jnp.float32)
    for h in range(heads):
        part, gain_part = unprepared(query_sum[:, h * HD : (h + 1) * HD], h * HD, gain[0:1, :])
        grads[:, h * HD : (h + 1) * HD] = part
        gain_grads[0:1, :] += gain_part
    for g in range(groups):
        columns = slice(g * HD, (g + 1) * HD)
        part, gain_part = unprepared(
            key_sum[:, columns] * scale, key_from + g * HD, gain[1:2, :]
        )
        grads[:, key_from + g * HD : key_from + (g + 1) * HD] = part
        gain_grads[1:2, :] += gain_part
        grads[:, value_from + g * HD : value_from + (g + 1) * HD] = value_sum[:, columns].astype(
            jnp.bfloat16
        )
    for i, near in enumerate(nears):
        grads_near[near, :] = grads[i * block : (i + 1) * block, :]


def attend_back(slots, gated_grad, raw, start, cosine, sine, gain, saved, heads, groups):
    length = raw.shape[0]
    query, key, value, attended, total_log = saved
    return pl.pallas_call(
        functools.partial(attend_back_kernel, heads, groups, length // slots.shape[0]),
        in_specs=in_vmem(11),
        out_shape=(
            jax.ShapeDtypeStruct(raw.shape, jnp.bfloat16),
            jax.ShapeDtypeStruct(raw.shape, jnp.bfloat16),
            jax.ShapeDtypeStruct((2, HD), jnp.float32),
        ),
        scratch_shapes=[
            pltpu.VMEM((length, heads * HD), jnp.bfloat16),
            pltpu.VMEM((length, HD), jnp.float32),
            pltpu.VMEM((length, heads * HD), jnp.float32),
            pltpu.VMEM((length, groups * HD), jnp.float32),
            pltpu.VMEM((length, groups * HD), jnp.float32),
        ],
        compiler_params=pltpu.CompilerParams(vmem_limit_bytes=56 * 2**20),
        cost_estimate=pl.CostEstimate(
            flops=10 * heads * length * length * HD,
            bytes_accessed=raw.size * 6 + length * heads * HD * 12,
            transcendentals=heads * length * length,
        ),
    )(slots, gated_grad, raw, start, cosine, sine, gain, query, key, value, attended, total_log)


def rope_tables(places):
    half = HD // 2
    freqs = ROPE_BASE ** (-2.0 * jnp.arange(half, dtype=jnp.float32) / HD)
    angles = places.astype(jnp.float32)[:, None] * freqs[None, :]
    cosine, sine = jnp.cos(angles), jnp.sin(angles)
    return jnp.concatenate([cosine, cosine], 1), jnp.concatenate([-sine, sine], 1)


def tie(*values):
    return lax.optimization_barrier(values)


TEAM = 4


def swapped(value, axis, flip):
    size = lax.axis_size(axis)
    return lax.ppermute(value, axis, [(i, i ^ flip) for i in range(size)])


def hop(value, axis):
    size = lax.axis_size(axis)
    return lax.ppermute(value, axis, [(i, (i - 1) % size) for i in range(size)])


def ring_gather(value, axis):
    pieces = [value]
    for _ in range(lax.axis_size(axis) - 1):
        pieces.append(hop(pieces[-1], axis))
    return pieces


def ring_scatter(parts, axis):
    size = lax.axis_size(axis)
    total = parts[1 % size]
    for step in range(1, size):
        total = parts[(step + 1) % size] + hop(total.astype(jnp.bfloat16), axis).astype(jnp.float32)
    return total


def wide_shape():
    size = lax.axis_size("w")
    return TEAM, size // TEAM


def wide_from(value, outer_step, inner_step):
    outer, inner = wide_shape()
    pairs = []
    for a in range(outer):
        for b in range(inner):
            source = (a + outer_step) % outer * inner + (b + inner_step) % inner
            pairs.append((source, a * inner + b))
    return lax.ppermute(value, "w", pairs)


def inner_gather(value):
    pieces = [value]
    for _ in range(wide_shape()[1] - 1):
        pieces.append(wide_from(pieces[-1], 0, 1))
    return pieces


def inner_scatter(parts):
    size = wide_shape()[1]
    total = parts[1 % size]
    for step in range(1, size):
        moved = wide_from(total.astype(jnp.bfloat16), 0, 1)
        total = parts[(step + 1) % size] + moved.astype(jnp.float32)
    return total


def wide_slots():
    outer, inner = wide_shape()
    me = lax.axis_index("w")
    a_me, b_me = me // inner, lax.rem(me, inner)
    return [
        [lax.rem(a_me + i, outer) * inner + lax.rem(b_me + j, inner) for j in range(inner)]
        for i in range(outer)
    ]


def outer_shift(value, step):
    return wide_from(value, step, 0)


def all_sum(value):
    for axis in ("x", "c", "w"):
        size = lax.axis_size(axis)
        step = 1
        while step < size:
            flips = [step, 2 * step, 3 * step] if 4 * step <= size else [step]
            moved = [value] + [swapped(value, axis, flip) for flip in flips]
            while len(moved) > 1:
                moved = [moved[i] + moved[i + 1] for i in range(0, len(moved), 2)]
            value = moved[0]
            step = step * (len(flips) + 1)
    return value


def assemble(pieces, axis):
    first = pieces[0][0]
    size = first.shape[axis]
    shape = list(first.shape)
    shape[axis] = size * len(pieces) * len(pieces[0])
    result = jnp.zeros(shape, first.dtype)
    for row, slots in zip(pieces, wide_slots()):
        for piece, slot in zip(row, slots):
            result = lax.dynamic_update_slice_in_dim(result, piece, slot * size, axis)
    return result


def near_slots():
    x_size = lax.axis_size("x")
    x_me, c_me = lax.axis_index("x"), lax.axis_index("c")
    return jnp.stack(
        [
            (core ^ c_me) * x_size + lax.rem(x + x_size - x_me, x_size)
            for x in range(x_size)
            for core in range(2)
        ]
    ).astype(jnp.int32)


def near_columns(values):
    x_size = lax.axis_size("x")
    x_me, c_me = lax.axis_index("x"), lax.axis_index("c")
    width = values.shape[1] // (2 * x_size)
    return jnp.concatenate(
        [
            lax.dynamic_slice_in_dim(
                values, (lax.rem(x_me + x, x_size) * 2 + (c_me ^ core)) * width, width, 1
            )
            for core in range(2)
            for x in range(x_size)
        ],
        1,
    )


def pinned(values):
    return with_layout_constraint(values, Layout(tuple(range(values.ndim))))


def by_x(total):
    x_size = lax.axis_size("x")
    rows = total.shape[0] // x_size
    return [total[i * rows : (i + 1) * rows] for i in range(x_size)]


def body(
    tokens,
    cotangent,
    segment_ids,
    domain_ids,
    domain_weights,
    gains,
    gain_first,
    gain_second,
    query_weight,
    query_first,
    query_second,
    keyvalue_weight,
    keyvalue_first,
    keyvalue_second,
    headgate_weight,
    headgate_first,
    headgate_second,
    output_weight,
    output_first,
    output_second,
    expand_weight,
    expand_first,
    expand_second,
    reduce_weight,
    reduce_first,
    reduce_second,
):
    head_devices = lax.axis_size("x") * lax.axis_size("c")
    core = lax.axis_index("c")
    outer, inner = wide_shape()
    heads = H // head_devices
    groups = KVH // head_devices
    low = jnp.bfloat16
    wide = jnp.float32
    labels = jnp.arange(NDOM, dtype=jnp.int32)
    onehot = domain_ids[:, None] == labels[None, :]
    token_weight = jnp.sum(jnp.where(onehot, domain_weights[None, :], 0.0), -1)
    upstream = cotangent.astype(wide) * token_weight[:, None]
    norm_one = gains[:D]
    norm_two = gains[D : 2 * D]
    head_gains = gains[2 * D :].reshape(2, HD)
    inputs = tokens.astype(wide)
    depth = query_weight.shape[0]
    query_width, key_width = query_weight.shape[1], keyvalue_weight.shape[2]
    value_from = query_width + key_width
    gate_from = value_from + key_width
    project = jnp.concatenate(
        [
            query_weight,
            keyvalue_weight[0],
            keyvalue_weight[1],
            headgate_weight,
            jnp.zeros((depth, -heads % 128), wide),
        ],
        1,
    ).astype(low)
    project, tokens_in = tie(project, tokens)
    normed = norm_rows(tokens_in.astype(wide), norm_one).astype(low)
    group_in = lax.all_gather(normed, ("x", "c"), axis=0, tiled=True)
    output_low = output_weight.astype(low)
    upstream_low = upstream.astype(low)
    hidden = reduce_weight.shape[0]

    def expand_whole(piece):
        return lax.all_gather(piece, ("x", "c"), axis=0, tiled=True)

    def reduce_whole(piece):
        return lax.all_gather(piece, ("x", "c"), axis=1, tiled=True)

    group_size = group_in.shape[0]
    places = positions(segment_ids)
    starts = (jnp.arange(group_size, dtype=jnp.int32) - places)[:, None]
    cosine, sine = rope_tables(places)

    near = near_slots()
    x_size = lax.axis_size("x")

    row = project
    project_pieces = []
    masters_in = (expand_weight, reduce_weight)
    for step in range(outer - 1):
        if step == 1:
            row, masters_in = tie(row, masters_in)
            expand_low = jnp.concatenate([masters_in[0][0], masters_in[0][1]], 1).astype(low)
            reduce_low = masters_in[1].astype(low)
            expand_all = [expand_whole(expand_low)]
            reduce_all = [reduce_whole(reduce_low)]
        moved, across, starts, cosine, sine = tie(
            wide_from(row, 1, 0), inner_gather(row), starts, cosine, sine
        )
        project_pieces.append(across)
        row = moved
    row, output_low, upstream_low = tie(row, output_low, upstream_low)
    output_rows = [output_low] + [wide_from(output_low, i, 0) for i in range(1, outer)]
    across, upstream_low, expand_low = tie(inner_gather(row), upstream_low, expand_low)
    project_pieces.append(across)
    project_all = assemble(project_pieces, 0)
    raw = jnp.dot(group_in, project_all, preferred_element_type=wide)
    raw, output_rows, expand_low, upstream_low = tie(raw, output_rows, expand_low, upstream_low)
    upstream_parts = [upstream_low, outer_shift(upstream_low, 1)]
    output_pieces = [inner_gather(piece) for piece in output_rows]
    kept = attend(near, raw, starts, cosine, sine, head_gains, heads, groups)
    kept, output_pieces, upstream_parts, expand_low = tie(
        kept, output_pieces, upstream_parts, expand_low
    )
    query, key, value, attended, total_log, gated, gated_near = kept
    expand_pieces = inner_gather(expand_low)
    upstream_parts.append(outer_shift(upstream_parts[-1], 1))
    output_all = assemble(output_pieces, 1)
    half = gated.shape[0] // 2

    def projected(rows):
        return jnp.dot(rows, output_all, preferred_element_type=wide)

    received = swapped(projected(gated_near[half:]).astype(low), "c", 1)
    attention = by_x(projected(gated_near[:half]) + received.astype(wide))
    split = attention[0].shape[0] // 2
    first = ring_scatter([part[:split] for part in attention], "x")
    second = ring_scatter([part[split:] for part in attention], "x")
    first, upstream_parts, expand_pieces, reduce_low = tie(
        first, upstream_parts, expand_pieces, reduce_low
    )
    expand_all = expand_all + [expand_whole(piece) for piece in expand_pieces[1:]]
    reduce_pieces = inner_gather(reduce_low)
    upstream_parts.append(outer_shift(upstream_parts[-1], 1))
    attention = jnp.concatenate([first, second], 0)
    residual = inputs + attention
    mixed = norm_rows(residual, norm_two).astype(low)

    def hidden_part(k, j):
        both = jnp.dot(mixed_parts[k], expand_all[j], preferred_element_type=wide)
        gate_pre, up_pre = both[:, :hidden], both[:, hidden:]
        activation = (jax.nn.silu(gate_pre) * up_pre).astype(low)
        activation_grad = contract_cols(upstream_parts[k], reduce_all[j])
        return activation, jnp.concatenate(swiglu_back(activation_grad, gate_pre, up_pre), 1)

    def mixed_back(parts, j):
        return contract_cols(parts[1], expand_all[j])

    def lowered(parts, j):
        return jnp.dot(parts[0], reduce_all[j], preferred_element_type=wide)

    done = {}
    grad_sums = {}

    def begin(k):
        done[k, 0] = hidden_part(k, 0)
        grad_sums[k] = mixed_back(done[k, 0], 0)

    def rest(k):
        for j in range(1, inner):
            done[k, j] = hidden_part(k, j)
            grad_sums[k] = grad_sums[k] + mixed_back(done[k, j], j)

    def summed(k):
        total = lowered(done[k, 0], 0)
        for j in range(1, inner):
            total = total + lowered(done[k, j], j)
        return total.astype(low) if k else total

    def joined(which, j):
        return jnp.concatenate([done[k, j][which] for k in range(outer)], 0)

    def expand_far(j):
        return contract_rows(mixed_near[:, D // 2 :], joined(1, j)).astype(low)

    def expand_term(j, x, far):
        rows = slice(x * D // head_devices, (x + 1) * D // head_devices)
        return contract_rows(mixed_near[:, rows], joined(1, j)) + far[rows].astype(wide)

    def reduce_far(j):
        return contract_rows(joined(0, j), upstream_near[:, D // 2 :]).astype(low)

    def reduce_term(j, x, far):
        columns = slice(x * D // head_devices, (x + 1) * D // head_devices)
        return contract_rows(joined(0, j), upstream_near[:, columns]) + far[:, columns].astype(wide)

    def x_finish(term, j, far, moved):
        for step in range(1, x_size):
            total = term(j, (step + 1) % x_size, far) + moved.astype(wide)
            if step + 1 < x_size:
                moved = hop(total.astype(low), "x")
        return total

    mixed_parts = [mixed]
    moved = outer_shift(mixed, 1)
    begin(0)
    moved, done, grad_sums, reduce_pieces, upstream_parts = tie(
        moved, done, grad_sums, reduce_pieces, upstream_parts
    )
    reduce_all = reduce_all + [reduce_whole(piece) for piece in reduce_pieces[1:]]
    mixed_parts.append(moved)
    moved = outer_shift(moved, 1)
    begin(1)
    upstream_all = jnp.concatenate(upstream_parts, 0)
    moved, done, grad_sums, upstream_all = tie(moved, done, grad_sums, upstream_all)
    mixed_parts.append(moved)
    moved = outer_shift(moved, 1)
    begin(2)
    rest(1)
    upstream_near = near_columns(upstream_all)
    moved, done, grad_sums, upstream_near = tie(moved, done, grad_sums, upstream_near)
    mixed_parts.append(moved)
    moved = outer_shift(grad_sums[1].astype(low), 1)
    rest(2)
    begin(3)
    mixed_all = jnp.concatenate(mixed_parts, 0)
    moved, done, grad_sums, mixed_all, mixed_parts = tie(
        moved, done, grad_sums, mixed_all, mixed_parts
    )
    moved = outer_shift((grad_sums[2] + moved.astype(wide)).astype(low), 1)
    rest(3)
    rest(0)
    moved, done, grad_sums, mixed_all, upstream_all = tie(
        moved, done, grad_sums, mixed_all, upstream_all
    )
    moved = outer_shift((grad_sums[3] + moved.astype(wide)).astype(low), 1)
    late = range(1, inner)
    mixed_near = near_columns(mixed_all)
    expand_fars = [None] + [expand_far(j) for j in late]
    output_sums = {1: summed(1)}
    expand_own = contract_rows(mixed_all, joined(1, 0)).astype(low)
    moved, done, mixed_near, expand_fars, output_sums, upstream_near, expand_own, upstream_all = tie(
        moved, done, mixed_near, expand_fars, output_sums, upstream_near, expand_own, upstream_all
    )
    mixed_grad = grad_sums[0] + moved.astype(wide)
    _, second_back = jax.vjp(norm_rows, residual, norm_two)
    residual_from, two_grad = second_back(mixed_grad)
    residual_grad = upstream + residual_from
    residual_row = ring_gather(residual_grad.astype(low), "x")
    output_total = outer_shift(output_sums[1], 1)
    expand_fars = [None] + [swapped(expand_fars[j], "c", 1) for j in late]
    expand_lead = [None] + [
        expand_term(j, 1 % x_size, expand_fars[j]).astype(low) for j in late
    ]
    reduce_fars = [None] + [reduce_far(j) for j in late]
    output_sums[2] = summed(2)
    output_sums[3] = summed(3)
    residual_row, output_total, expand_fars, expand_lead, reduce_fars, done, output_sums = tie(
        residual_row, output_total, expand_fars, expand_lead, reduce_fars, done, output_sums
    )
    residual_far = [swapped(piece, "c", 1) for piece in residual_row]
    reduce_fars = [None] + [swapped(reduce_fars[j], "c", 1) for j in late]
    expand_moved = [None] + [hop(expand_lead[j], "x") for j in late]
    residual_all = jnp.concatenate(residual_row + residual_far, 0)
    residual_all, reduce_fars, done = tie(residual_all, reduce_fars, done)
    slots = wide_slots()

    def wide_parts(whole, axis, i):
        return [lax.dynamic_slice_in_dim(whole, slot * depth, depth, axis) for slot in slots[i]]

    order = [(step + 1) % outer for step in range(outer)]

    def output_rows_of(i):
        return jnp.concatenate(wide_parts(output_grad, 1, i), 1)

    gated_grad = contract_cols(residual_all, output_all)
    output_total = outer_shift(output_sums[2] + output_total, 1)
    back = attend_back(
        near,
        gated_grad,
        raw,
        starts,
        cosine,
        sine,
        head_gains,
        (query, key, value, attended, total_log),
        heads,
        groups,
    )
    back, output_total, done, residual_all, expand_moved, expand_own, upstream_all = tie(
        back, output_total, done, residual_all, expand_moved, expand_own, upstream_all
    )
    expand_own = lax.psum_scatter(expand_own, ("x", "c"), scatter_dimension=0, tiled=True)
    low_grads, low_near, head_gain_grads = back

    def normed_back(rows):
        return contract_cols(rows, project_all)

    output_total = outer_shift(output_sums[3] + output_total, 1)
    project_grad = pinned(contract_rows(group_in, low_grads))
    project_grad, low_near, done, upstream_all, residual_all, expand_moved, reduce_fars = tie(
        project_grad, low_near, done, upstream_all, residual_all, expand_moved, reduce_fars
    )

    def spread(parts):
        total = parts[0]
        for part in parts[1:]:
            total = (part.astype(wide) + wide_from(total, 0, 1).astype(wide)).astype(low)
        return wide_from(total, 0, 1)

    project_total = inner_scatter(wide_parts(project_grad, 0, order[0]))
    output_grad = contract_rows(gated_near, residual_all)
    output_part = output_rows_of(order[0])
    expand_wide = [
        x_finish(expand_term, j, expand_fars[j], expand_moved[j]) for j in late
    ]
    reduce_lead = [None] + [
        reduce_term(j, 1 % x_size, reduce_fars[j]).astype(low) for j in late
    ]
    middle = len(expand_wide[0]) // 2
    expand_early = [part[:middle].astype(low) for part in expand_wide]
    expand_late = [part[middle:].astype(low) for part in expand_wide]
    normed_far = normed_back(low_near[half:]).astype(low)
    state = (project_total, output_part, output_grad, expand_early, expand_late, reduce_lead)
    state, project_grad, low_near, done, upstream_all, normed_far, output_total = tie(
        state, project_grad, low_near, done, upstream_all, normed_far, output_total
    )
    project_total, output_part, output_grad, expand_early, expand_late, reduce_lead = state
    for step, i in enumerate(order[1:]):
        moved = outer_shift(project_total.astype(low), 1)
        across = inner_scatter(wide_parts(project_grad, 0, i))
        output_new = outer_shift(output_part.astype(low), 1)
        if step == 0:
            normed_far = swapped(normed_far, "c", 1)
            reduce_moved = [None] + [hop(reduce_lead[j], "x") for j in late]
            expand_early = spread(expand_early)
            normed_grad = normed_back(low_near[:half]) + normed_far.astype(wide)
            reduce_own = contract_rows(joined(0, 0), upstream_all).astype(low)
            reduce_wide = ()
        if step == 1:
            reduce_own = lax.psum_scatter(reduce_own, ("x", "c"), scatter_dimension=1, tiled=True)
            normed_grad = ring_scatter(by_x(normed_grad), "x")
            expand_late = spread(expand_late)
            reduce_wide = [
                x_finish(reduce_term, j, reduce_fars[j], reduce_moved[j]).astype(low) for j in late
            ]
        if step == 2:
            reduce_wide = spread(reduce_wide)
        state = (moved, across, project_grad, output_new, output_grad, reduce_wide)
        if step == 0:
            state, expand_early, reduce_own, reduce_moved, expand_late, normed_grad = tie(
                state, expand_early, reduce_own, reduce_moved, expand_late, normed_grad
            )
        elif step == 1:
            state, expand_own, expand_late = tie(state, expand_own, expand_late)
        else:
            state, normed_grad = tie(state, normed_grad)
        moved, across, project_grad, output_new, output_grad, reduce_wide = state
        project_total = across + moved.astype(wide)
        output_part = output_rows_of(i) + output_new.astype(wide)
    output_part = inner_scatter([output_part[:, j * depth : (j + 1) * depth] for j in range(inner)])
    expand_both = jnp.concatenate([expand_early, expand_late], 0).astype(wide)
    expand_both = expand_both + expand_own.astype(wide)
    reduce_part = reduce_wide.astype(wide) + reduce_own.astype(wide)
    project_part = pinned(project_total)
    block_output = (residual + summed(0) + output_total.astype(wide)).astype(low)
    _, first_back = jax.vjp(norm_rows, inputs, norm_one)
    input_from, one_grad = first_back(normed_grad)
    input_grad = residual_grad + input_from
    expand_part = jnp.stack([expand_both[:, :hidden], expand_both[:, hidden:]])
    query_part = project_part[:, :query_width]
    keyvalue_part = jnp.stack(
        [project_part[:, query_width:value_from], project_part[:, value_from:gate_from]]
    )
    headgate_part = pinned(project_part[:, gate_from : gate_from + heads].T)
    gain_partial = jnp.concatenate([one_grad, two_grad, head_gain_grads.reshape(-1)])
    parts = (query_part, keyvalue_part, headgate_part, output_part, expand_part, reduce_part)
    squares = jnp.zeros((), jnp.float32)
    for part_grad in parts:
        squares = squares + jnp.sum(part_grad * part_grad)
    totals = jnp.concatenate([gain_partial, squares[None]])
    totals = all_sum(totals)
    gains_grad, square_total = totals[:-1], totals[-1]
    grad_norm = jnp.sqrt(square_total + jnp.sum(gains_grad * gains_grad))
    clip = CLIP_NORM / jnp.maximum(grad_norm, CLIP_NORM)
    gains_new = adam_step(gains, gains_grad * clip, gain_first, gain_second, GAIN_RATE, 0.0)
    masters = (
        query_weight,
        keyvalue_weight,
        headgate_weight.T,
        output_weight,
        expand_weight,
        reduce_weight,
    )
    states = (
        (query_first, query_second),
        (keyvalue_first, keyvalue_second),
        (headgate_first.T, headgate_second.T),
        (output_first, output_second),
        (expand_first, expand_second),
        (reduce_first, reduce_second),
    )
    results = [grad_norm, block_output, input_grad, gains_new[0], gains_new[1], gains_new[2]]
    for index in range(6):
        rate = OUTPUT_RATE if index == 3 else WEIGHT_RATE
        updated, first_new, second_new = adam_step(
            masters[index],
            parts[index] * clip,
            states[index][0],
            states[index][1],
            rate,
            WEIGHT_DECAY,
        )
        made = [updated, first_new, second_new, updated.astype(low)]
        results = results + ([item.T for item in made] if index == 2 else made)
    return tuple(results)


def solution(mesh):
    heads, wides = mesh.shape["head"], mesh.shape["wide"]
    grid = Mesh(mesh.devices.reshape(heads // 2, 2, wides), ("x", "c", "w"))
    wide, head = ("w",), ("x", "c")
    rows = P(wide + head, None)
    by_wide = P(wide, head)
    stacked = P(None, wide, head)
    by_head = P(head, wide)
    widened = P(None, head, wide)
    return jax.shard_map(
        body,
        mesh=grid,
        in_specs=(rows, rows, P(wide), P(wide + head))
        + (P(),) * 4
        + (by_wide,) * 3
        + (stacked,) * 3
        + (by_wide,) * 3
        + (by_head,) * 3
        + (widened,) * 3
        + (by_wide,) * 3,
        out_specs=(P(), rows, rows)
        + (P(),) * 3
        + (by_wide,) * 4
        + (stacked,) * 4
        + (by_wide,) * 4
        + (by_head,) * 4
        + (widened,) * 4
        + (by_wide,) * 4,
        check_vma=False,
    )
```

```python
import functools

import jax
import jax.numpy as jnp
from jax import lax
from jax.experimental import pallas as pl
from jax.experimental.layout import Layout, with_layout_constraint
from jax.experimental.pallas import tpu as pltpu
from jax.sharding import Mesh
from jax.sharding import PartitionSpec as P

D = 2048
H = 16
HD = 128
KVH = 8
NDOM = 8
STEP = 10


NORM_EPS = 1e-06
ROPE_BASE = 1000000.0
MASK_FILL = -1e30
CLIP_NORM = 1.0
WEIGHT_RATE = 0.02
OUTPUT_RATE = 0.12
GAIN_RATE = 0.7
BETA_FIRST = 0.9
BETA_SECOND = 0.95
ADAM_EPS = 1e-08
WEIGHT_DECAY = 0.1
LOG2E = 1.4426950408889634


def rms_scale(values):
    return values * lax.rsqrt(jnp.mean(values * values, -1, keepdims=True) + NORM_EPS)


def norm_rows(values, gain):
    return rms_scale(values) * gain


def positions(segments):
    length = segments.shape[0]
    places = jnp.arange(length, dtype=jnp.int32)
    starts = jnp.concatenate([jnp.ones((1,), dtype=bool), segments[1:] != segments[:-1]])
    return places - lax.cummax(jnp.where(starts, places, 0), axis=0)


def contract_rows(left, right):
    return lax.dot_general(
        left, right, (((0,), (0,)), ((), ())), preferred_element_type=jnp.float32
    )


def contract_cols(left, right):
    return lax.dot_general(
        left, right, (((1,), (1,)), ((), ())), preferred_element_type=jnp.float32
    )


def swiglu_back(activation_grad, gate_pre, up_pre):
    gate_sigmoid = jax.nn.sigmoid(gate_pre)
    gate_grad = (
        activation_grad * up_pre * gate_sigmoid * (1.0 + gate_pre * (1.0 - gate_sigmoid))
    ).astype(jnp.bfloat16)
    up_grad = (activation_grad * gate_pre * gate_sigmoid).astype(jnp.bfloat16)
    return (gate_grad, up_grad)


def adam_step(weight, grad, first, second, rate, decay):
    first_new = BETA_FIRST * first + (1.0 - BETA_FIRST) * grad
    second_new = BETA_SECOND * second + (1.0 - BETA_SECOND) * grad * grad
    first_hat = first_new / (1.0 - BETA_FIRST**STEP)
    second_hat = second_new / (1.0 - BETA_SECOND**STEP)
    updated = weight - rate * (first_hat / (jnp.sqrt(second_hat) + ADAM_EPS) + decay * weight)
    return (updated, first_new, second_new)


def turn(values, cosine, sine):
    return values * cosine + pltpu.roll(values, HD // 2, 1) * sine


def lane_mean(values):
    ones = jnp.full((HD, HD), 1.0 / HD, jnp.bfloat16)
    return jnp.dot(values.astype(jnp.bfloat16), ones, preferred_element_type=jnp.float32)


def dot_cols(left, right):
    return lax.dot_general(
        left, right, (((1,), (1,)), ((), ())), preferred_element_type=jnp.float32
    )


def dot_rows(left, right):
    return lax.dot_general(
        left, right, (((0,), (0,)), ((), ())), preferred_element_type=jnp.float32
    )


def allowed_queries(start, first, block, length, repeat):
    keys = lax.broadcasted_iota(jnp.int32, (length, block), 0)
    queries = first + lax.broadcasted_iota(jnp.int32, (length, block), 1)
    allowed = (keys >= start) & (keys <= queries)
    return jnp.concatenate([allowed] * repeat, 1)


def allowed_keys(start, first, block, length, repeat):
    keys = lax.broadcasted_iota(jnp.int32, (block, length), 1)
    queries = first + lax.broadcasted_iota(jnp.int32, (block, length), 0)
    allowed = (keys >= start) & (keys <= queries)
    return jnp.concatenate([allowed] * repeat, 0)


def attend_kernel(
    heads,
    groups,
    block,
    slots,
    raw,
    start,
    cosine,
    sine,
    gain,
    query,
    key,
    value,
    attended,
    total_log,
    gated,
    gated_near,
):
    length = raw.shape[0]
    repeat = heads // groups
    key_from, value_from, gate_from = heads * HD, (heads + groups) * HD, (heads + 2 * groups) * HD
    cos, sin = cosine[...], sine[...]

    def prepared(column, gain_row):
        part = raw[:, column : column + HD]
        scale = lax.rsqrt(lane_mean(part * part) + NORM_EPS)
        return turn(part * scale * gain_row, cos, sin).astype(jnp.bfloat16)

    for g in range(groups):
        key[:, g * HD : (g + 1) * HD] = prepared(key_from + g * HD, gain[1:2, :])
        value[:, g * HD : (g + 1) * HD] = raw[
            :, value_from + g * HD : value_from + (g + 1) * HD
        ].astype(jnp.bfloat16)
    for h in range(heads):
        query[:, h * HD : (h + 1) * HD] = prepared(h * HD, gain[0:1, :])
    total_log[...] = jnp.zeros(total_log.shape, jnp.float32)
    for i in range(length // block):
        rows = slice(i * block, (i + 1) * block)
        near = pl.ds(pl.multiple_of(slots[i] * block, block), block)
        seen = (i + 1) * block
        mask = allowed_keys(start[rows, :], i * block, block, seen, repeat)
        for g in range(groups):
            columns = slice(g * HD, (g + 1) * HD)
            hs = range(g * repeat, (g + 1) * repeat)
            queries = jnp.concatenate([query[rows, h * HD : (h + 1) * HD] for h in hs], 0)
            scores = dot_cols(queries, key[:seen, columns]) * (HD**-0.5 * LOG2E)
            exponent = jnp.exp2(jnp.where(mask, scores, MASK_FILL))
            total = jnp.sum(exponent, -1, keepdims=True)
            result = jnp.dot(
                exponent.astype(jnp.bfloat16), value[:seen, columns], preferred_element_type=jnp.float32
            ) / total
            logs = jnp.log2(total)
            for r, h in enumerate(hs):
                part = result[r * block : (r + 1) * block, :]
                gate = jax.nn.sigmoid(raw[rows, gate_from + h : gate_from + h + 1])
                attended[rows, h * HD : (h + 1) * HD] = part
                part_low = (part * gate).astype(jnp.bfloat16)
                gated[rows, h * HD : (h + 1) * HD] = part_low
                gated_near[near, h * HD : (h + 1) * HD] = part_low
                total_log[rows, h : h + 1] = logs[r * block : (r + 1) * block, :]


def in_vmem(count):
    return [pl.BlockSpec(memory_space=pltpu.SMEM)] + [pl.BlockSpec(memory_space=pltpu.VMEM)] * count


def attend(slots, raw, start, cosine, sine, gain, heads, groups):
    length = raw.shape[0]
    low = jnp.bfloat16
    return pl.pallas_call(
        functools.partial(attend_kernel, heads, groups, length // slots.shape[0]),
        in_specs=in_vmem(5),
        out_shape=(
            jax.ShapeDtypeStruct((length, heads * HD), low),
            jax.ShapeDtypeStruct((length, groups * HD), low),
            jax.ShapeDtypeStruct((length, groups * HD), low),
            jax.ShapeDtypeStruct((length, heads * HD), jnp.float32),
            jax.ShapeDtypeStruct((length, HD), jnp.float32),
            jax.ShapeDtypeStruct((length, heads * HD), low),
            jax.ShapeDtypeStruct((length, heads * HD), low),
        ),
        compiler_params=pltpu.CompilerParams(vmem_limit_bytes=56 * 2**20),
        cost_estimate=pl.CostEstimate(
            flops=4 * heads * length * length * HD,
            bytes_accessed=raw.size * 4 + length * heads * HD * 10,
            transcendentals=heads * length * length,
        ),
    )(slots, raw, start, cosine, sine, gain)


def attend_back_kernel(
    heads,
    groups,
    block,
    slots,
    gated_grad,
    raw_all,
    start,
    cosine_all,
    sine_all,
    gain,
    query,
    key,
    value,
    attended,
    total_log,
    grads,
    grads_near,
    gain_grads,
    low_grad,
    delta,
    query_sum,
    key_sum,
    value_sum,
    raw,
    gates,
    cosine,
    sine,
    copied,
):
    length = raw.shape[0]
    repeat = heads // groups
    key_from, value_from, gate_from = heads * HD, (heads + groups) * HD, (heads + 2 * groups) * HD
    scale = HD**-0.5
    copies = [
        pltpu.make_async_copy(raw_all.at[:, gate_from : gate_from + HD], gates, copied.at[0]),
        pltpu.make_async_copy(raw_all.at[:, :value_from], raw, copied.at[1]),
        pltpu.make_async_copy(cosine_all, cosine, copied.at[2]),
        pltpu.make_async_copy(sine_all, sine, copied.at[3]),
    ]
    for copy in copies:
        copy.start()
    nears = [
        pl.ds(pl.multiple_of(slots[i] * block, block), block) for i in range(length // block)
    ]

    def unprepared(grad, column, gain_row):
        part = raw[:, column : column + HD]
        inverse = lax.rsqrt(lane_mean(part * part) + NORM_EPS)
        unit = part * inverse
        back = grad * cos - pltpu.roll(grad, HD // 2, 1) * sin
        inner = back * gain_row
        result = inverse * (inner - unit * lane_mean(inner * unit))
        return result.astype(jnp.bfloat16), jnp.sum(back * unit, 0, keepdims=True)

    grads[:, gate_from:] = jnp.zeros((length, grads.shape[1] - gate_from), jnp.bfloat16)
    copies[0].wait()
    for h in range(heads):
        columns = slice(h * HD, (h + 1) * HD)
        gate = jax.nn.sigmoid(gates[:, h : h + 1])
        outer = jnp.concatenate([gated_grad[near, columns] for near in nears], 0)
        result = attended[:, columns]
        low = (outer * gate).astype(jnp.bfloat16)
        low_grad[:, columns] = low
        logit = jnp.sum(outer * result, -1, keepdims=True) * gate * (1.0 - gate)
        grads[:, gate_from + h : gate_from + h + 1] = logit.astype(jnp.bfloat16)
        delta[:, h : h + 1] = jnp.sum(low.astype(jnp.float32) * result, -1, keepdims=True)
    key_sum[...] = jnp.zeros(key_sum.shape, jnp.float32)
    value_sum[...] = jnp.zeros(value_sum.shape, jnp.float32)
    log_rows = jnp.transpose(total_log[...])
    delta_rows = jnp.transpose(delta[...])
    for i in range(length // block):
        rows = slice(i * block, (i + 1) * block)
        seen = (i + 1) * block
        mask = allowed_queries(start[0:1, rows], i * block, block, seen, repeat)
        for g in range(groups):
            columns = slice(g * HD, (g + 1) * HD)
            hs = range(g * repeat, (g + 1) * repeat)
            queries = jnp.concatenate([query[rows, h * HD : (h + 1) * HD] for h in hs], 0)
            outers = jnp.concatenate([low_grad[rows, h * HD : (h + 1) * HD] for h in hs], 0)
            logs = jnp.concatenate([log_rows[h : h + 1, rows] for h in hs], 1)
            deltas = jnp.concatenate([delta_rows[h : h + 1, rows] for h in hs], 1)
            keys, values = key[:seen, columns], value[:seen, columns]
            scores = dot_cols(keys, queries) * (scale * LOG2E)
            probs = jnp.exp2(jnp.where(mask, scores - logs, MASK_FILL))
            prob_grad = dot_cols(values, outers)
            score_grad = (probs * (prob_grad - deltas)).astype(jnp.bfloat16)
            moved = dot_rows(score_grad, keys) * scale
            for r, h in enumerate(hs):
                query_sum[rows, h * HD : (h + 1) * HD] = moved[r * block : (r + 1) * block, :]
            key_sum[:seen, columns] += jnp.dot(
                score_grad, queries, preferred_element_type=jnp.float32
            )
            value_sum[:seen, columns] += jnp.dot(
                probs.astype(jnp.bfloat16), outers, preferred_element_type=jnp.float32
            )
    gain_grads[...] = jnp.zeros(gain_grads.shape, jnp.float32)
    for copy in copies[1:]:
        copy.wait()
    cos, sin = cosine[...], sine[...]
    for h in range(heads):
        part, gain_part = unprepared(query_sum[:, h * HD : (h + 1) * HD], h * HD, gain[0:1, :])
        grads[:, h * HD : (h + 1) * HD] = part
        gain_grads[0:1, :] += gain_part
    for g in range(groups):
        columns = slice(g * HD, (g + 1) * HD)
        part, gain_part = unprepared(
            key_sum[:, columns] * scale, key_from + g * HD, gain[1:2, :]
        )
        grads[:, key_from + g * HD : key_from + (g + 1) * HD] = part
        gain_grads[1:2, :] += gain_part
        grads[:, value_from + g * HD : value_from + (g + 1) * HD] = value_sum[:, columns].astype(
            jnp.bfloat16
        )
    for i, near in enumerate(nears):
        grads_near[near, :] = grads[i * block : (i + 1) * block, :]


def attend_back(slots, gated_grad, raw, start, cosine, sine, gain, saved, heads, groups):
    length = raw.shape[0]
    query, key, value, attended, total_log = saved
    return pl.pallas_call(
        functools.partial(attend_back_kernel, heads, groups, length // slots.shape[0]),
        in_specs=[
            pl.BlockSpec(memory_space=pl.ANY) if i in (2, 4, 5) else spec
            for i, spec in enumerate(in_vmem(11))
        ],
        out_shape=(
            jax.ShapeDtypeStruct(raw.shape, jnp.bfloat16),
            jax.ShapeDtypeStruct(raw.shape, jnp.bfloat16),
            jax.ShapeDtypeStruct((2, HD), jnp.float32),
        ),
        scratch_shapes=[
            pltpu.VMEM((length, heads * HD), jnp.bfloat16),
            pltpu.VMEM((length, HD), jnp.float32),
            pltpu.VMEM((length, heads * HD), jnp.float32),
            pltpu.VMEM((length, groups * HD), jnp.float32),
            pltpu.VMEM((length, groups * HD), jnp.float32),
            pltpu.VMEM((length, (heads + groups) * HD), jnp.float32),
            pltpu.VMEM((length, HD), jnp.float32),
            pltpu.VMEM((length, HD), jnp.float32),
            pltpu.VMEM((length, HD), jnp.float32),
            pltpu.SemaphoreType.DMA((4,)),
        ],
        compiler_params=pltpu.CompilerParams(vmem_limit_bytes=56 * 2**20),
        cost_estimate=pl.CostEstimate(
            flops=10 * heads * length * length * HD,
            bytes_accessed=raw.size * 6 + length * heads * HD * 12,
            transcendentals=heads * length * length,
        ),
    )(slots, gated_grad, raw, start, cosine, sine, gain, query, key, value, attended, total_log)


def rope_tables(places):
    half = HD // 2
    freqs = ROPE_BASE ** (-2.0 * jnp.arange(half, dtype=jnp.float32) / HD)
    angles = places.astype(jnp.float32)[:, None] * freqs[None, :]
    cosine, sine = jnp.cos(angles), jnp.sin(angles)
    return jnp.concatenate([cosine, cosine], 1), jnp.concatenate([-sine, sine], 1)


def tie(*values):
    return lax.optimization_barrier(values)


TEAM = 4


def swapped(value, axis, flip):
    size = lax.axis_size(axis)
    return lax.ppermute(value, axis, [(i, i ^ flip) for i in range(size)])


def hop(value, axis):
    size = lax.axis_size(axis)
    return lax.ppermute(value, axis, [(i, (i - 1) % size) for i in range(size)])


def ring_gather(value, axis):
    pieces = [value]
    for _ in range(lax.axis_size(axis) - 1):
        pieces.append(hop(pieces[-1], axis))
    return pieces


def ring_scatter(parts, axis):
    size = lax.axis_size(axis)
    total = parts[1 % size]
    for step in range(1, size):
        total = parts[(step + 1) % size] + hop(total.astype(jnp.bfloat16), axis).astype(jnp.float32)
    return total


def wide_shape():
    size = lax.axis_size("w")
    return TEAM, size // TEAM


def wide_from(value, outer_step, inner_step):
    outer, inner = wide_shape()
    pairs = []
    for a in range(outer):
        for b in range(inner):
            source = (a + outer_step) % outer * inner + (b + inner_step) % inner
            pairs.append((source, a * inner + b))
    return lax.ppermute(value, "w", pairs)


def inner_gather(value):
    pieces = [value]
    for _ in range(wide_shape()[1] - 1):
        pieces.append(wide_from(pieces[-1], 0, 1))
    return pieces


def inner_scatter(parts):
    size = wide_shape()[1]
    total = parts[1 % size]
    for step in range(1, size):
        moved = wide_from(total.astype(jnp.bfloat16), 0, 1)
        total = parts[(step + 1) % size] + moved.astype(jnp.float32)
    return total


def wide_slots():
    outer, inner = wide_shape()
    me = lax.axis_index("w")
    a_me, b_me = me // inner, lax.rem(me, inner)
    return [
        [lax.rem(a_me + i, outer) * inner + lax.rem(b_me + j, inner) for j in range(inner)]
        for i in range(outer)
    ]


def outer_shift(value, step):
    return wide_from(value, step, 0)


def all_sum(value):
    for axis in ("x", "c", "w"):
        size = lax.axis_size(axis)
        step = 1
        while step < size:
            flips = [step, 2 * step, 3 * step] if 4 * step <= size else [step]
            moved = [value] + [swapped(value, axis, flip) for flip in flips]
            while len(moved) > 1:
                moved = [moved[i] + moved[i + 1] for i in range(0, len(moved), 2)]
            value = moved[0]
            step = step * (len(flips) + 1)
    return value


def assemble(pieces, axis):
    first = pieces[0][0]
    size = first.shape[axis]
    shape = list(first.shape)
    shape[axis] = size * len(pieces) * len(pieces[0])
    result = jnp.zeros(shape, first.dtype)
    for row, slots in zip(pieces, wide_slots()):
        for piece, slot in zip(row, slots):
            result = lax.dynamic_update_slice_in_dim(result, piece, slot * size, axis)
    return result


def near_slots():
    x_size = lax.axis_size("x")
    x_me, c_me = lax.axis_index("x"), lax.axis_index("c")
    return jnp.stack(
        [
            (core ^ c_me) * x_size + lax.rem(x + x_size - x_me, x_size)
            for x in range(x_size)
            for core in range(2)
        ]
    ).astype(jnp.int32)


def near_columns(values):
    x_size = lax.axis_size("x")
    x_me, c_me = lax.axis_index("x"), lax.axis_index("c")
    width = values.shape[1] // (2 * x_size)
    return jnp.concatenate(
        [
            lax.dynamic_slice_in_dim(
                values, (lax.rem(x_me + x, x_size) * 2 + (c_me ^ core)) * width, width, 1
            )
            for core in range(2)
            for x in range(x_size)
        ],
        1,
    )


def pinned(values):
    return with_layout_constraint(values, Layout(tuple(range(values.ndim))))


def by_x(total):
    x_size = lax.axis_size("x")
    rows = total.shape[0] // x_size
    return [total[i * rows : (i + 1) * rows] for i in range(x_size)]


def body(
    tokens,
    cotangent,
    segment_ids,
    domain_ids,
    domain_weights,
    gains,
    gain_first,
    gain_second,
    query_weight,
    query_first,
    query_second,
    keyvalue_weight,
    keyvalue_first,
    keyvalue_second,
    headgate_weight,
    headgate_first,
    headgate_second,
    output_weight,
    output_first,
    output_second,
    expand_weight,
    expand_first,
    expand_second,
    reduce_weight,
    reduce_first,
    reduce_second,
):
    head_devices = lax.axis_size("x") * lax.axis_size("c")
    core = lax.axis_index("c")
    outer, inner = wide_shape()
    heads = H // head_devices
    groups = KVH // head_devices
    low = jnp.bfloat16
    wide = jnp.float32
    labels = jnp.arange(NDOM, dtype=jnp.int32)
    onehot = domain_ids[:, None] == labels[None, :]
    token_weight = jnp.sum(jnp.where(onehot, domain_weights[None, :], 0.0), -1)
    upstream = cotangent.astype(wide) * token_weight[:, None]
    norm_one = gains[:D]
    norm_two = gains[D : 2 * D]
    head_gains = gains[2 * D :].reshape(2, HD)
    inputs = tokens.astype(wide)
    depth = query_weight.shape[0]
    query_width, key_width = query_weight.shape[1], keyvalue_weight.shape[2]
    value_from = query_width + key_width
    gate_from = value_from + key_width
    project = jnp.concatenate(
        [
            query_weight,
            keyvalue_weight[0],
            keyvalue_weight[1],
            headgate_weight,
            jnp.zeros((depth, -heads % 128), wide),
        ],
        1,
    ).astype(low)
    project, tokens_in = tie(project, tokens)
    normed = norm_rows(tokens_in.astype(wide), norm_one).astype(low)
    group_in = lax.all_gather(normed, ("x", "c"), axis=0, tiled=True)
    output_low = output_weight.astype(low)
    upstream_low = upstream.astype(low)
    hidden = reduce_weight.shape[0]

    def expand_whole(piece):
        return lax.all_gather(piece, ("x", "c"), axis=0, tiled=True)

    def reduce_whole(piece):
        return lax.all_gather(piece, ("x", "c"), axis=1, tiled=True)

    group_size = group_in.shape[0]
    places = positions(segment_ids)
    starts = jnp.arange(group_size, dtype=jnp.int32) - places
    starts = (starts[:, None], starts[None, :])
    cosine, sine = rope_tables(places)

    near = near_slots()
    x_size = lax.axis_size("x")

    row = project
    project_pieces = []
    masters_in = (expand_weight, reduce_weight)
    for step in range(outer - 1):
        if step == 1:
            row, masters_in = tie(row, masters_in)
            expand_low = jnp.concatenate([masters_in[0][0], masters_in[0][1]], 1).astype(low)
            reduce_low = masters_in[1].astype(low)
            expand_all = [expand_whole(expand_low)]
            reduce_all = [reduce_whole(reduce_low)]
        moved, across, starts, cosine, sine, head_gains = tie(
            wide_from(row, 1, 0), inner_gather(row), starts, cosine, sine, head_gains
        )
        project_pieces.append(across)
        row = moved
    row, output_low, upstream_low = tie(row, output_low, upstream_low)
    output_rows = [output_low] + [wide_from(output_low, i, 0) for i in range(1, outer)]
    across, upstream_low, expand_low = tie(inner_gather(row), upstream_low, expand_low)
    project_pieces.append(across)
    project_all = assemble(project_pieces, 0)
    raw = jnp.dot(group_in, project_all, preferred_element_type=wide)
    output_pair = inner_gather(output_low)
    raw, output_rows, expand_low, upstream_low, output_pair = tie(
        raw, output_rows, expand_low, upstream_low, output_pair
    )
    upstream_parts = [upstream_low, outer_shift(upstream_low, 1)]
    output_pieces = [output_pair] + [inner_gather(piece) for piece in output_rows[1:]]
    kept = attend(near, raw, starts[0], cosine, sine, head_gains, heads, groups)
    kept, output_pieces, upstream_parts, expand_low = tie(
        kept, output_pieces, upstream_parts, expand_low
    )
    query, key, value, attended, total_log, gated, gated_near = kept
    expand_pieces = inner_gather(expand_low)
    upstream_parts.append(outer_shift(upstream_parts[-1], 1))
    output_all = assemble(output_pieces, 1)
    half = gated.shape[0] // 2

    def projected(rows):
        return jnp.dot(rows, output_all, preferred_element_type=wide)

    received = swapped(projected(gated_near[half:]).astype(low), "c", 1)
    attention = by_x(projected(gated_near[:half]) + received.astype(wide))
    split = attention[0].shape[0] // 2
    first = ring_scatter([part[:split] for part in attention], "x")
    second = ring_scatter([part[split:] for part in attention], "x")
    first, upstream_parts, expand_pieces, reduce_low = tie(
        first, upstream_parts, expand_pieces, reduce_low
    )
    expand_all = expand_all + [expand_whole(piece) for piece in expand_pieces[1:]]
    reduce_pieces = inner_gather(reduce_low)
    upstream_parts.append(outer_shift(upstream_parts[-1], 1))
    attention = jnp.concatenate([first, second], 0)
    residual = inputs + attention
    mixed = norm_rows(residual, norm_two).astype(low)

    def hidden_part(k, j):
        both = jnp.dot(mixed_parts[k], expand_all[j], preferred_element_type=wide)
        gate_pre, up_pre = both[:, :hidden], both[:, hidden:]
        activation = (jax.nn.silu(gate_pre) * up_pre).astype(low)
        activation_grad = contract_cols(upstream_parts[k], reduce_all[j])
        return activation, jnp.concatenate(swiglu_back(activation_grad, gate_pre, up_pre), 1)

    def mixed_back(parts, j):
        return contract_cols(parts[1], expand_all[j])

    def lowered(parts, j):
        return jnp.dot(parts[0], reduce_all[j], preferred_element_type=wide)

    done = {}
    grad_sums = {}

    def begin(k):
        done[k, 0] = hidden_part(k, 0)
        grad_sums[k] = mixed_back(done[k, 0], 0)

    def rest(k):
        for j in range(1, inner):
            done[k, j] = hidden_part(k, j)
            grad_sums[k] = grad_sums[k] + mixed_back(done[k, j], j)

    def summed(k):
        total = lowered(done[k, 0], 0)
        for j in range(1, inner):
            total = total + lowered(done[k, j], j)
        return total.astype(low) if k else total

    def joined(which, j):
        return jnp.concatenate([done[k, j][which] for k in range(outer)], 0)

    def expand_far(j):
        return contract_rows(mixed_near[:, D // 2 :], joined(1, j)).astype(low)

    def expand_term(j, x, far):
        rows = slice(x * D // head_devices, (x + 1) * D // head_devices)
        return contract_rows(mixed_near[:, rows], joined(1, j)) + far[rows].astype(wide)

    def reduce_far(j):
        return contract_rows(joined(0, j), upstream_near[:, D // 2 :]).astype(low)

    def reduce_term(j, x, far):
        columns = slice(x * D // head_devices, (x + 1) * D // head_devices)
        return contract_rows(joined(0, j), upstream_near[:, columns]) + far[:, columns].astype(wide)

    def x_finish(term, j, far, moved):
        for step in range(1, x_size):
            total = term(j, (step + 1) % x_size, far) + moved.astype(wide)
            if step + 1 < x_size:
                moved = hop(total.astype(low), "x")
        return total

    mixed_parts = [mixed]
    moved = outer_shift(mixed, 1)
    begin(0)
    moved, done, grad_sums, reduce_pieces, upstream_parts = tie(
        moved, done, grad_sums, reduce_pieces, upstream_parts
    )
    reduce_all = reduce_all + [reduce_whole(piece) for piece in reduce_pieces[1:]]
    mixed_parts.append(moved)
    moved = outer_shift(moved, 1)
    begin(1)
    upstream_all = jnp.concatenate(upstream_parts, 0)
    moved, done, grad_sums, upstream_all = tie(moved, done, grad_sums, upstream_all)
    mixed_parts.append(moved)
    moved = outer_shift(moved, 1)
    begin(2)
    rest(1)
    moved, done, grad_sums = tie(moved, done, grad_sums)
    mixed_parts.append(moved)
    moved = outer_shift(grad_sums[1].astype(low), 1)
    rest(2)
    begin(3)
    mixed_all = jnp.concatenate(mixed_parts, 0)
    moved, done, grad_sums, mixed_all, mixed_parts = tie(
        moved, done, grad_sums, mixed_all, mixed_parts
    )
    moved = outer_shift((grad_sums[2] + moved.astype(wide)).astype(low), 1)
    rest(3)
    rest(0)
    moved, done, grad_sums, mixed_all, upstream_all = tie(
        moved, done, grad_sums, mixed_all, upstream_all
    )
    moved = outer_shift((grad_sums[3] + moved.astype(wide)).astype(low), 1)
    late = range(1, inner)
    mixed_near = near_columns(mixed_all)
    expand_fars = [None] + [expand_far(j) for j in late]
    output_sums = {1: summed(1)}
    expand_own = contract_rows(mixed_all, joined(1, 0)).astype(low)
    moved, done, mixed_near, expand_fars, output_sums, expand_own, upstream_all = tie(
        moved, done, mixed_near, expand_fars, output_sums, expand_own, upstream_all
    )
    mixed_grad = grad_sums[0] + moved.astype(wide)
    _, second_back = jax.vjp(norm_rows, residual, norm_two)
    residual_from, two_grad = second_back(mixed_grad)
    residual_grad = upstream + residual_from
    residual_row = ring_gather(residual_grad.astype(low), "x")
    output_total = outer_shift(output_sums[1], 1)
    expand_fars = [None] + [swapped(expand_fars[j], "c", 1) for j in late]
    expand_lead = [None] + [
        expand_term(j, 1 % x_size, expand_fars[j]).astype(low) for j in late
    ]
    upstream_near = near_columns(upstream_all)
    reduce_fars = [None] + [reduce_far(j) for j in late]
    output_sums[2] = summed(2)
    output_sums[3] = summed(3)
    residual_row, output_total, expand_fars, expand_lead, reduce_fars, done, output_sums = tie(
        residual_row, output_total, expand_fars, expand_lead, reduce_fars, done, output_sums
    )
    residual_far = [swapped(piece, "c", 1) for piece in residual_row]
    reduce_fars = [None] + [swapped(reduce_fars[j], "c", 1) for j in late]
    expand_moved = [None] + [hop(expand_lead[j], "x") for j in late]
    residual_all = jnp.concatenate(residual_row + residual_far, 0)
    residual_all, reduce_fars, done = tie(residual_all, reduce_fars, done)
    slots = wide_slots()

    def wide_parts(whole, axis, i):
        return [lax.dynamic_slice_in_dim(whole, slot * depth, depth, axis) for slot in slots[i]]

    order = [(step + 1) % outer for step in range(outer)]

    def output_rows_of(i):
        return jnp.concatenate(wide_parts(output_grad, 1, i), 1)

    gated_grad = contract_cols(residual_all, output_all)
    output_total = outer_shift(output_sums[2] + output_total, 1)
    back = attend_back(
        near,
        gated_grad,
        raw,
        starts[1],
        cosine,
        sine,
        head_gains,
        (query, key, value, attended, total_log),
        heads,
        groups,
    )
    back, output_total, done, residual_all, expand_moved, expand_own, upstream_all = tie(
        back, output_total, done, residual_all, expand_moved, expand_own, upstream_all
    )
    expand_own = lax.psum_scatter(expand_own, ("x", "c"), scatter_dimension=0, tiled=True)
    low_grads, low_near, head_gain_grads = back

    def normed_back(rows):
        return contract_cols(rows, project_all)

    project_grad = pinned(contract_rows(group_in, low_grads))
    project_grad, low_near, done, upstream_all, residual_all, expand_moved, reduce_fars, output_total = tie(
        project_grad, low_near, done, upstream_all, residual_all, expand_moved, reduce_fars, output_total
    )
    output_total = outer_shift(output_sums[3] + output_total, 1)

    def spread(parts):
        total = parts[0]
        for part in parts[1:]:
            total = (part.astype(wide) + wide_from(total, 0, 1).astype(wide)).astype(low)
        return wide_from(total, 0, 1)

    project_total = inner_scatter(wide_parts(project_grad, 0, order[0]))
    output_grad = contract_rows(gated_near, residual_all)
    output_part = output_rows_of(order[0])
    expand_wide = [
        x_finish(expand_term, j, expand_fars[j], expand_moved[j]) for j in late
    ]
    reduce_lead = [None] + [
        reduce_term(j, 1 % x_size, reduce_fars[j]).astype(low) for j in late
    ]
    middle = len(expand_wide[0]) // 2
    expand_early = [part[:middle].astype(low) for part in expand_wide]
    expand_late = [part[middle:].astype(low) for part in expand_wide]
    normed_far = normed_back(low_near[half:]).astype(low)
    state = (project_total, output_part, output_grad, expand_early, expand_late, reduce_lead)
    state, project_grad, low_near, done, upstream_all, normed_far, output_total = tie(
        state, project_grad, low_near, done, upstream_all, normed_far, output_total
    )
    project_total, output_part, output_grad, expand_early, expand_late, reduce_lead = state
    for step, i in enumerate(order[1:]):
        moved = outer_shift(project_total.astype(low), 1)
        across = inner_scatter(wide_parts(project_grad, 0, i))
        output_new = outer_shift(output_part.astype(low), 1)
        if step == 0:
            normed_far = swapped(normed_far, "c", 1)
            reduce_moved = [None] + [hop(reduce_lead[j], "x") for j in late]
            expand_early = spread(expand_early)
            normed_parts = []
            width = half // x_size
            for x in range(x_size):
                block = slice(x * width, (x + 1) * width)
                part = normed_back(low_near[block]) + normed_far[block].astype(wide)
                normed_parts.append(part.astype(low) if x == 1 else part)
            reduce_own = contract_rows(joined(0, 0), upstream_all).astype(low)
            reduce_wide = ()
        if step == 1:
            reduce_own = lax.psum_scatter(reduce_own, ("x", "c"), scatter_dimension=1, tiled=True)
            normed_moved = hop(normed_parts[1 % x_size], "x")
            expand_late = spread(expand_late)
            reduce_wide = [
                x_finish(reduce_term, j, reduce_fars[j], reduce_moved[j]).astype(low) for j in late
            ]
        if step == 2:
            reduce_wide = spread(reduce_wide)
        state = (moved, across, project_grad, output_new, output_grad, reduce_wide)
        if step == 0:
            state, expand_early, reduce_own, reduce_moved, expand_late, normed_parts = tie(
                state, expand_early, reduce_own, reduce_moved, expand_late, normed_parts
            )
        elif step == 1:
            state, expand_own, expand_late = tie(state, expand_own, expand_late)
        else:
            state, normed_moved, normed_parts = tie(state, normed_moved, normed_parts)
        moved, across, project_grad, output_new, output_grad, reduce_wide = state
        project_total = across + moved.astype(wide)
        output_part = output_rows_of(i) + output_new.astype(wide)
    output_part = inner_scatter([output_part[:, j * depth : (j + 1) * depth] for j in range(inner)])
    for step in range(1, x_size):
        normed_grad = normed_parts[(step + 1) % x_size] + normed_moved.astype(wide)
        if step + 1 < x_size:
            normed_moved = hop(normed_grad.astype(low), "x")
    expand_both = jnp.concatenate([expand_early, expand_late], 0).astype(wide)
    expand_both = expand_both + expand_own.astype(wide)
    reduce_part = reduce_wide.astype(wide) + reduce_own.astype(wide)
    project_part = pinned(project_total)
    block_output = (residual + summed(0) + output_total.astype(wide)).astype(low)
    _, first_back = jax.vjp(norm_rows, inputs, norm_one)
    input_from, one_grad = first_back(normed_grad)
    input_grad = residual_grad + input_from
    expand_part = jnp.stack([expand_both[:, :hidden], expand_both[:, hidden:]])
    query_part = project_part[:, :query_width]
    keyvalue_part = jnp.stack(
        [project_part[:, query_width:value_from], project_part[:, value_from:gate_from]]
    )
    headgate_part = pinned(project_part[:, gate_from : gate_from + heads].T)
    gain_partial = jnp.concatenate([one_grad, two_grad, head_gain_grads.reshape(-1)])
    parts = (query_part, keyvalue_part, headgate_part, output_part, expand_part, reduce_part)
    squares = jnp.zeros((), jnp.float32)
    for part_grad in parts:
        squares = squares + jnp.sum(part_grad * part_grad)
    totals = jnp.concatenate([gain_partial, squares[None]])
    totals = all_sum(totals)
    gains_grad, square_total = totals[:-1], totals[-1]
    grad_norm = jnp.sqrt(square_total + jnp.sum(gains_grad * gains_grad))
    clip = CLIP_NORM / jnp.maximum(grad_norm, CLIP_NORM)
    gains_new = adam_step(gains, gains_grad * clip, gain_first, gain_second, GAIN_RATE, 0.0)
    masters = (
        query_weight,
        keyvalue_weight,
        headgate_weight.T,
        output_weight,
        expand_weight,
        reduce_weight,
    )
    states = (
        (query_first, query_second),
        (keyvalue_first, keyvalue_second),
        (headgate_first.T, headgate_second.T),
        (output_first, output_second),
        (expand_first, expand_second),
        (reduce_first, reduce_second),
    )
    results = [grad_norm, block_output, input_grad, gains_new[0], gains_new[1], gains_new[2]]
    for index in range(6):
        rate = OUTPUT_RATE if index == 3 else WEIGHT_RATE
        updated, first_new, second_new = adam_step(
            masters[index],
            parts[index] * clip,
            states[index][0],
            states[index][1],
            rate,
            WEIGHT_DECAY,
        )
        made = [updated, first_new, second_new, updated.astype(low)]
        results = results + ([item.T for item in made] if index == 2 else made)
    return tuple(results)


def solution(mesh):
    heads, wides = mesh.shape["head"], mesh.shape["wide"]
    grid = Mesh(mesh.devices.reshape(heads // 2, 2, wides), ("x", "c", "w"))
    wide, head = ("w",), ("x", "c")
    rows = P(wide + head, None)
    by_wide = P(wide, head)
    stacked = P(None, wide, head)
    by_head = P(head, wide)
    widened = P(None, head, wide)
    return jax.shard_map(
        body,
        mesh=grid,
        in_specs=(rows, rows, P(wide), P(wide + head))
        + (P(),) * 4
        + (by_wide,) * 3
        + (stacked,) * 3
        + (by_wide,) * 3
        + (by_head,) * 3
        + (widened,) * 3
        + (by_wide,) * 3,
        out_specs=(P(), rows, rows)
        + (P(),) * 3
        + (by_wide,) * 4
        + (stacked,) * 4
        + (by_wide,) * 4
        + (by_head,) * 4
        + (widened,) * 4
        + (by_wide,) * 4,
        check_vma=False,
    )
```

```python
import functools

import jax
import jax.numpy as jnp
from jax import lax
from jax.experimental import pallas as pl
from jax.experimental.layout import Layout, with_layout_constraint
from jax.experimental.pallas import tpu as pltpu
from jax.sharding import Mesh
from jax.sharding import PartitionSpec as P

D = 2048
H = 16
HD = 128
KVH = 8
NDOM = 8
STEP = 10


NORM_EPS = 1e-06
ROPE_BASE = 1000000.0
MASK_FILL = -1e30
CLIP_NORM = 1.0
WEIGHT_RATE = 0.02
OUTPUT_RATE = 0.12
GAIN_RATE = 0.7
BETA_FIRST = 0.9
BETA_SECOND = 0.95
ADAM_EPS = 1e-08
WEIGHT_DECAY = 0.1
LOG2E = 1.4426950408889634


def rms_scale(values):
    return values * lax.rsqrt(jnp.mean(values * values, -1, keepdims=True) + NORM_EPS)


def norm_rows(values, gain):
    return rms_scale(values) * gain


def positions(segments):
    length = segments.shape[0]
    places = jnp.arange(length, dtype=jnp.int32)
    starts = jnp.concatenate([jnp.ones((1,), dtype=bool), segments[1:] != segments[:-1]])
    return places - lax.cummax(jnp.where(starts, places, 0), axis=0)


def contract_rows(left, right):
    return lax.dot_general(
        left, right, (((0,), (0,)), ((), ())), preferred_element_type=jnp.float32
    )


def contract_cols(left, right):
    return lax.dot_general(
        left, right, (((1,), (1,)), ((), ())), preferred_element_type=jnp.float32
    )


def swiglu_back(activation_grad, gate_pre, up_pre):
    gate_sigmoid = jax.nn.sigmoid(gate_pre)
    gate_grad = (
        activation_grad * up_pre * gate_sigmoid * (1.0 + gate_pre * (1.0 - gate_sigmoid))
    ).astype(jnp.bfloat16)
    up_grad = (activation_grad * gate_pre * gate_sigmoid).astype(jnp.bfloat16)
    return (gate_grad, up_grad)


def adam_step(weight, grad, first, second, rate, decay):
    first_new = BETA_FIRST * first + (1.0 - BETA_FIRST) * grad
    second_new = BETA_SECOND * second + (1.0 - BETA_SECOND) * grad * grad
    first_hat = first_new / (1.0 - BETA_FIRST**STEP)
    second_hat = second_new / (1.0 - BETA_SECOND**STEP)
    updated = weight - rate * (first_hat / (jnp.sqrt(second_hat) + ADAM_EPS) + decay * weight)
    return (updated, first_new, second_new)


def turn(values, cosine, sine):
    return values * cosine + pltpu.roll(values, HD // 2, 1) * sine


def lane_mean(values):
    ones = jnp.full((HD, HD), 1.0 / HD, jnp.bfloat16)
    return jnp.dot(values.astype(jnp.bfloat16), ones, preferred_element_type=jnp.float32)


def dot_cols(left, right):
    return lax.dot_general(
        left, right, (((1,), (1,)), ((), ())), preferred_element_type=jnp.float32
    )


def dot_rows(left, right):
    return lax.dot_general(
        left, right, (((0,), (0,)), ((), ())), preferred_element_type=jnp.float32
    )


def allowed_queries(start, first, block, length, repeat):
    keys = lax.broadcasted_iota(jnp.int32, (length, block), 0)
    queries = first + lax.broadcasted_iota(jnp.int32, (length, block), 1)
    allowed = (keys >= start) & (keys <= queries)
    return jnp.concatenate([allowed] * repeat, 1)


def allowed_keys(start, first, block, length, repeat):
    keys = lax.broadcasted_iota(jnp.int32, (block, length), 1)
    queries = first + lax.broadcasted_iota(jnp.int32, (block, length), 0)
    allowed = (keys >= start) & (keys <= queries)
    return jnp.concatenate([allowed] * repeat, 0)


def attend_kernel(
    heads,
    groups,
    block,
    slots,
    raw,
    start,
    cosine,
    sine,
    gain,
    query,
    key,
    value,
    attended,
    total_log,
    gated,
    gated_near,
):
    length = raw.shape[0]
    repeat = heads // groups
    key_from, value_from, gate_from = heads * HD, (heads + groups) * HD, (heads + 2 * groups) * HD
    cos, sin = cosine[...], sine[...]

    def prepared(column, gain_row):
        part = raw[:, column : column + HD]
        scale = lax.rsqrt(lane_mean(part * part) + NORM_EPS)
        return turn(part * scale * gain_row, cos, sin).astype(jnp.bfloat16)

    for g in range(groups):
        key[:, g * HD : (g + 1) * HD] = prepared(key_from + g * HD, gain[1:2, :])
        value[:, g * HD : (g + 1) * HD] = raw[
            :, value_from + g * HD : value_from + (g + 1) * HD
        ].astype(jnp.bfloat16)
    for h in range(heads):
        query[:, h * HD : (h + 1) * HD] = prepared(h * HD, gain[0:1, :])
    total_log[...] = jnp.zeros(total_log.shape, jnp.float32)
    for i in range(length // block):
        rows = slice(i * block, (i + 1) * block)
        near = pl.ds(pl.multiple_of(slots[i] * block, block), block)
        seen = (i + 1) * block
        mask = allowed_keys(start[rows, :], i * block, block, seen, repeat)
        for g in range(groups):
            columns = slice(g * HD, (g + 1) * HD)
            hs = range(g * repeat, (g + 1) * repeat)
            queries = jnp.concatenate([query[rows, h * HD : (h + 1) * HD] for h in hs], 0)
            scores = dot_cols(queries, key[:seen, columns]) * (HD**-0.5 * LOG2E)
            exponent = jnp.exp2(jnp.where(mask, scores, MASK_FILL))
            total = jnp.sum(exponent, -1, keepdims=True)
            result = jnp.dot(
                exponent.astype(jnp.bfloat16), value[:seen, columns], preferred_element_type=jnp.float32
            ) / total
            logs = jnp.log2(total)
            for r, h in enumerate(hs):
                part = result[r * block : (r + 1) * block, :]
                gate = jax.nn.sigmoid(raw[rows, gate_from + h : gate_from + h + 1])
                attended[rows, h * HD : (h + 1) * HD] = part
                part_low = (part * gate).astype(jnp.bfloat16)
                gated[rows, h * HD : (h + 1) * HD] = part_low
                gated_near[near, h * HD : (h + 1) * HD] = part_low
                total_log[rows, h : h + 1] = logs[r * block : (r + 1) * block, :]


def in_vmem(count):
    return [pl.BlockSpec(memory_space=pltpu.SMEM)] + [pl.BlockSpec(memory_space=pltpu.VMEM)] * count


def attend(slots, raw, start, cosine, sine, gain, heads, groups):
    length = raw.shape[0]
    low = jnp.bfloat16
    return pl.pallas_call(
        functools.partial(attend_kernel, heads, groups, length // slots.shape[0]),
        in_specs=in_vmem(5),
        out_shape=(
            jax.ShapeDtypeStruct((length, heads * HD), low),
            jax.ShapeDtypeStruct((length, groups * HD), low),
            jax.ShapeDtypeStruct((length, groups * HD), low),
            jax.ShapeDtypeStruct((length, heads * HD), jnp.float32),
            jax.ShapeDtypeStruct((length, HD), jnp.float32),
            jax.ShapeDtypeStruct((length, heads * HD), low),
            jax.ShapeDtypeStruct((length, heads * HD), low),
        ),
        compiler_params=pltpu.CompilerParams(vmem_limit_bytes=56 * 2**20),
        cost_estimate=pl.CostEstimate(
            flops=4 * heads * length * length * HD,
            bytes_accessed=raw.size * 4 + length * heads * HD * 10,
            transcendentals=heads * length * length,
        ),
    )(slots, raw, start, cosine, sine, gain)


def attend_back_kernel(
    heads,
    groups,
    block,
    slots,
    gated_grad,
    raw_all,
    start,
    cosine_all,
    sine_all,
    gain,
    query,
    key,
    value,
    attended,
    total_log,
    grads,
    grads_near,
    gain_grads,
    low_grad,
    delta,
    query_sum,
    key_sum,
    value_sum,
    raw,
    gates,
    cosine,
    sine,
    copied,
):
    length = raw.shape[0]
    repeat = heads // groups
    key_from, value_from, gate_from = heads * HD, (heads + groups) * HD, (heads + 2 * groups) * HD
    scale = HD**-0.5
    copies = [
        pltpu.make_async_copy(raw_all.at[:, gate_from : gate_from + HD], gates, copied.at[0]),
        pltpu.make_async_copy(raw_all.at[:, :value_from], raw, copied.at[1]),
        pltpu.make_async_copy(cosine_all, cosine, copied.at[2]),
        pltpu.make_async_copy(sine_all, sine, copied.at[3]),
    ]
    for copy in copies:
        copy.start()
    nears = [
        pl.ds(pl.multiple_of(slots[i] * block, block), block) for i in range(length // block)
    ]

    def unprepared(grad, column, gain_row):
        part = raw[:, column : column + HD]
        inverse = lax.rsqrt(lane_mean(part * part) + NORM_EPS)
        unit = part * inverse
        back = grad * cos - pltpu.roll(grad, HD // 2, 1) * sin
        inner = back * gain_row
        result = inverse * (inner - unit * lane_mean(inner * unit))
        return result.astype(jnp.bfloat16), jnp.sum(back * unit, 0, keepdims=True)

    grads[:, gate_from:] = jnp.zeros((length, grads.shape[1] - gate_from), jnp.bfloat16)
    copies[0].wait()
    for h in range(heads):
        columns = slice(h * HD, (h + 1) * HD)
        gate = jax.nn.sigmoid(gates[:, h : h + 1])
        outer = jnp.concatenate([gated_grad[near, columns] for near in nears], 0)
        result = attended[:, columns]
        low = (outer * gate).astype(jnp.bfloat16)
        low_grad[:, columns] = low
        logit = jnp.sum(outer * result, -1, keepdims=True) * gate * (1.0 - gate)
        grads[:, gate_from + h : gate_from + h + 1] = logit.astype(jnp.bfloat16)
        delta[:, h : h + 1] = jnp.sum(low.astype(jnp.float32) * result, -1, keepdims=True)
    key_sum[...] = jnp.zeros(key_sum.shape, jnp.float32)
    value_sum[...] = jnp.zeros(value_sum.shape, jnp.float32)
    log_rows = jnp.transpose(total_log[...])
    delta_rows = jnp.transpose(delta[...])
    for i in range(length // block):
        rows = slice(i * block, (i + 1) * block)
        seen = (i + 1) * block
        mask = allowed_queries(start[0:1, rows], i * block, block, seen, repeat)
        for g in range(groups):
            columns = slice(g * HD, (g + 1) * HD)
            hs = range(g * repeat, (g + 1) * repeat)
            queries = jnp.concatenate([query[rows, h * HD : (h + 1) * HD] for h in hs], 0)
            outers = jnp.concatenate([low_grad[rows, h * HD : (h + 1) * HD] for h in hs], 0)
            logs = jnp.concatenate([log_rows[h : h + 1, rows] for h in hs], 1)
            deltas = jnp.concatenate([delta_rows[h : h + 1, rows] for h in hs], 1)
            keys, values = key[:seen, columns], value[:seen, columns]
            scores = dot_cols(keys, queries) * (scale * LOG2E)
            probs = jnp.exp2(jnp.where(mask, scores - logs, MASK_FILL))
            prob_grad = dot_cols(values, outers)
            score_grad = (probs * (prob_grad - deltas)).astype(jnp.bfloat16)
            moved = dot_rows(score_grad, keys) * scale
            for r, h in enumerate(hs):
                query_sum[rows, h * HD : (h + 1) * HD] = moved[r * block : (r + 1) * block, :]
            key_sum[:seen, columns] += jnp.dot(
                score_grad, queries, preferred_element_type=jnp.float32
            )
            value_sum[:seen, columns] += jnp.dot(
                probs.astype(jnp.bfloat16), outers, preferred_element_type=jnp.float32
            )
    gain_grads[...] = jnp.zeros(gain_grads.shape, jnp.float32)
    for copy in copies[1:]:
        copy.wait()
    cos, sin = cosine[...], sine[...]
    for h in range(heads):
        part, gain_part = unprepared(query_sum[:, h * HD : (h + 1) * HD], h * HD, gain[0:1, :])
        grads[:, h * HD : (h + 1) * HD] = part
        gain_grads[0:1, :] += gain_part
    for g in range(groups):
        columns = slice(g * HD, (g + 1) * HD)
        part, gain_part = unprepared(
            key_sum[:, columns] * scale, key_from + g * HD, gain[1:2, :]
        )
        grads[:, key_from + g * HD : key_from + (g + 1) * HD] = part
        gain_grads[1:2, :] += gain_part
        grads[:, value_from + g * HD : value_from + (g + 1) * HD] = value_sum[:, columns].astype(
            jnp.bfloat16
        )
    for i, near in enumerate(nears):
        grads_near[near, :] = grads[i * block : (i + 1) * block, :]


def attend_back(slots, gated_grad, raw, start, cosine, sine, gain, saved, heads, groups):
    length = raw.shape[0]
    query, key, value, attended, total_log = saved
    return pl.pallas_call(
        functools.partial(attend_back_kernel, heads, groups, length // slots.shape[0]),
        in_specs=[
            pl.BlockSpec(memory_space=pl.ANY) if i in (2, 4, 5) else spec
            for i, spec in enumerate(in_vmem(11))
        ],
        out_shape=(
            jax.ShapeDtypeStruct(raw.shape, jnp.bfloat16),
            jax.ShapeDtypeStruct(raw.shape, jnp.bfloat16),
            jax.ShapeDtypeStruct((2, HD), jnp.float32),
        ),
        scratch_shapes=[
            pltpu.VMEM((length, heads * HD), jnp.bfloat16),
            pltpu.VMEM((length, HD), jnp.float32),
            pltpu.VMEM((length, heads * HD), jnp.float32),
            pltpu.VMEM((length, groups * HD), jnp.float32),
            pltpu.VMEM((length, groups * HD), jnp.float32),
            pltpu.VMEM((length, (heads + groups) * HD), jnp.float32),
            pltpu.VMEM((length, HD), jnp.float32),
            pltpu.VMEM((length, HD), jnp.float32),
            pltpu.VMEM((length, HD), jnp.float32),
            pltpu.SemaphoreType.DMA((4,)),
        ],
        compiler_params=pltpu.CompilerParams(vmem_limit_bytes=56 * 2**20),
        cost_estimate=pl.CostEstimate(
            flops=10 * heads * length * length * HD,
            bytes_accessed=raw.size * 6 + length * heads * HD * 12,
            transcendentals=heads * length * length,
        ),
    )(slots, gated_grad, raw, start, cosine, sine, gain, query, key, value, attended, total_log)


def rope_tables(places):
    half = HD // 2
    freqs = ROPE_BASE ** (-2.0 * jnp.arange(half, dtype=jnp.float32) / HD)
    angles = places.astype(jnp.float32)[:, None] * freqs[None, :]
    cosine, sine = jnp.cos(angles), jnp.sin(angles)
    return jnp.concatenate([cosine, cosine], 1), jnp.concatenate([-sine, sine], 1)


def tie(*values):
    return lax.optimization_barrier(values)


TEAM = 4


def swapped(value, axis, flip):
    size = lax.axis_size(axis)
    return lax.ppermute(value, axis, [(i, i ^ flip) for i in range(size)])


def hop(value, axis):
    size = lax.axis_size(axis)
    return lax.ppermute(value, axis, [(i, (i - 1) % size) for i in range(size)])


def ring_gather(value, axis):
    pieces = [value]
    for _ in range(lax.axis_size(axis) - 1):
        pieces.append(hop(pieces[-1], axis))
    return pieces


def ring_scatter(parts, axis):
    size = lax.axis_size(axis)
    total = parts[1 % size]
    for step in range(1, size):
        total = parts[(step + 1) % size] + hop(total.astype(jnp.bfloat16), axis).astype(jnp.float32)
    return total


def wide_shape():
    size = lax.axis_size("w")
    return TEAM, size // TEAM


def wide_from(value, outer_step, inner_step):
    outer, inner = wide_shape()
    pairs = []
    for a in range(outer):
        for b in range(inner):
            source = (a + outer_step) % outer * inner + (b + inner_step) % inner
            pairs.append((source, a * inner + b))
    return lax.ppermute(value, "w", pairs)


def inner_gather(value):
    pieces = [value]
    for _ in range(wide_shape()[1] - 1):
        pieces.append(wide_from(pieces[-1], 0, 1))
    return pieces


def inner_scatter(parts):
    size = wide_shape()[1]
    total = parts[1 % size]
    for step in range(1, size):
        moved = wide_from(total.astype(jnp.bfloat16), 0, 1)
        total = parts[(step + 1) % size] + moved.astype(jnp.float32)
    return total


def wide_slots():
    outer, inner = wide_shape()
    me = lax.axis_index("w")
    a_me, b_me = me // inner, lax.rem(me, inner)
    return [
        [lax.rem(a_me + i, outer) * inner + lax.rem(b_me + j, inner) for j in range(inner)]
        for i in range(outer)
    ]


def outer_shift(value, step):
    return wide_from(value, step, 0)


def all_sum(value):
    for axis in ("x", "c", "w"):
        size = lax.axis_size(axis)
        step = 1
        while step < size:
            flips = [step, 2 * step, 3 * step] if 4 * step <= size else [step]
            moved = [value] + [swapped(value, axis, flip) for flip in flips]
            while len(moved) > 1:
                moved = [moved[i] + moved[i + 1] for i in range(0, len(moved), 2)]
            value = moved[0]
            step = step * (len(flips) + 1)
    return value


def assemble(pieces, axis):
    first = pieces[0][0]
    size = first.shape[axis]
    shape = list(first.shape)
    shape[axis] = size * len(pieces) * len(pieces[0])
    result = jnp.zeros(shape, first.dtype)
    for row, slots in zip(pieces, wide_slots()):
        for piece, slot in zip(row, slots):
            result = lax.dynamic_update_slice_in_dim(result, piece, slot * size, axis)
    return result


def near_slots():
    x_size = lax.axis_size("x")
    x_me, c_me = lax.axis_index("x"), lax.axis_index("c")
    return jnp.stack(
        [
            (core ^ c_me) * x_size + lax.rem(x + x_size - x_me, x_size)
            for x in range(x_size)
            for core in range(2)
        ]
    ).astype(jnp.int32)


def near_columns(values):
    x_size = lax.axis_size("x")
    x_me, c_me = lax.axis_index("x"), lax.axis_index("c")
    width = values.shape[1] // (2 * x_size)
    return jnp.concatenate(
        [
            lax.dynamic_slice_in_dim(
                values, (lax.rem(x_me + x, x_size) * 2 + (c_me ^ core)) * width, width, 1
            )
            for core in range(2)
            for x in range(x_size)
        ],
        1,
    )


def pinned(values):
    return with_layout_constraint(values, Layout(tuple(range(values.ndim))))


def by_x(total):
    x_size = lax.axis_size("x")
    rows = total.shape[0] // x_size
    return [total[i * rows : (i + 1) * rows] for i in range(x_size)]


def body(
    tokens,
    cotangent,
    segment_ids,
    domain_ids,
    domain_weights,
    gains,
    gain_first,
    gain_second,
    query_weight,
    query_first,
    query_second,
    keyvalue_weight,
    keyvalue_first,
    keyvalue_second,
    headgate_weight,
    headgate_first,
    headgate_second,
    output_weight,
    output_first,
    output_second,
    expand_weight,
    expand_first,
    expand_second,
    reduce_weight,
    reduce_first,
    reduce_second,
):
    head_devices = lax.axis_size("x") * lax.axis_size("c")
    core = lax.axis_index("c")
    outer, inner = wide_shape()
    heads = H // head_devices
    groups = KVH // head_devices
    low = jnp.bfloat16
    wide = jnp.float32
    labels = jnp.arange(NDOM, dtype=jnp.int32)
    onehot = domain_ids[:, None] == labels[None, :]
    token_weight = jnp.sum(jnp.where(onehot, domain_weights[None, :], 0.0), -1)
    upstream = cotangent.astype(wide) * token_weight[:, None]
    norm_one = gains[:D]
    norm_two = gains[D : 2 * D]
    head_gains = gains[2 * D :].reshape(2, HD)
    inputs = tokens.astype(wide)
    depth = query_weight.shape[0]
    query_width, key_width = query_weight.shape[1], keyvalue_weight.shape[2]
    value_from = query_width + key_width
    gate_from = value_from + key_width
    project = jnp.concatenate(
        [
            query_weight,
            keyvalue_weight[0],
            keyvalue_weight[1],
            headgate_weight,
            jnp.zeros((depth, -heads % 128), wide),
        ],
        1,
    ).astype(low)
    project, tokens_in = tie(project, tokens)
    normed = norm_rows(tokens_in.astype(wide), norm_one).astype(low)
    group_in = lax.all_gather(normed, ("x", "c"), axis=0, tiled=True)
    output_low = output_weight.astype(low)
    upstream_low = upstream.astype(low)
    hidden = reduce_weight.shape[0]

    def expand_whole(piece):
        return lax.all_gather(piece, ("x", "c"), axis=0, tiled=True)

    def reduce_whole(piece):
        return lax.all_gather(piece, ("x", "c"), axis=1, tiled=True)

    group_size = group_in.shape[0]
    places = positions(segment_ids)
    starts = jnp.arange(group_size, dtype=jnp.int32) - places
    starts = (starts[:, None], starts[None, :])
    cosine, sine = rope_tables(places)

    near = near_slots()
    x_size = lax.axis_size("x")

    row = project
    project_pieces = []
    masters_in = (expand_weight, reduce_weight)
    for step in range(outer - 1):
        if step == 1:
            row, masters_in = tie(row, masters_in)
            expand_low = jnp.concatenate([masters_in[0][0], masters_in[0][1]], 1).astype(low)
            reduce_low = masters_in[1].astype(low)
            expand_all = [expand_whole(expand_low)]
            reduce_all = [reduce_whole(reduce_low)]
        moved, across, starts, cosine, sine, head_gains = tie(
            wide_from(row, 1, 0), inner_gather(row), starts, cosine, sine, head_gains
        )
        project_pieces.append(across)
        row = moved
    row, output_low, upstream_low = tie(row, output_low, upstream_low)
    output_rows = [output_low] + [wide_from(output_low, i, 0) for i in range(1, outer)]
    across, upstream_low, expand_low = tie(inner_gather(row), upstream_low, expand_low)
    project_pieces.append(across)
    project_all = assemble(project_pieces, 0)
    raw = jnp.dot(group_in, project_all, preferred_element_type=wide)
    output_pair = inner_gather(output_low)
    raw, output_rows, expand_low, upstream_low, output_pair = tie(
        raw, output_rows, expand_low, upstream_low, output_pair
    )
    upstream_parts = [upstream_low, outer_shift(upstream_low, 1)]
    output_pieces = [output_pair] + [inner_gather(piece) for piece in output_rows[1:]]
    kept = attend(near, raw, starts[0], cosine, sine, head_gains, heads, groups)
    kept, output_pieces, upstream_parts, expand_low = tie(
        kept, output_pieces, upstream_parts, expand_low
    )
    query, key, value, attended, total_log, gated, gated_near = kept
    expand_pieces = inner_gather(expand_low)
    upstream_parts.append(outer_shift(upstream_parts[-1], 1))
    output_all = assemble(output_pieces, 1)
    half = gated.shape[0] // 2

    def projected(rows):
        return jnp.dot(rows, output_all, preferred_element_type=wide)

    received = swapped(projected(gated_near[half:]).astype(low), "c", 1)
    attention = by_x(projected(gated_near[:half]) + received.astype(wide))
    split = attention[0].shape[0] // 2
    first = ring_scatter([part[:split] for part in attention], "x")
    second = ring_scatter([part[split:] for part in attention], "x")
    first, upstream_parts, expand_pieces, reduce_low = tie(
        first, upstream_parts, expand_pieces, reduce_low
    )
    expand_all = expand_all + [expand_whole(piece) for piece in expand_pieces[1:]]
    reduce_pieces = inner_gather(reduce_low)
    upstream_parts.append(outer_shift(upstream_parts[-1], 1))
    attention = jnp.concatenate([first, second], 0)
    residual = inputs + attention
    mixed = norm_rows(residual, norm_two).astype(low)

    def hidden_part(k, j):
        both = jnp.dot(mixed_parts[k], expand_all[j], preferred_element_type=wide)
        gate_pre, up_pre = both[:, :hidden], both[:, hidden:]
        activation = (jax.nn.silu(gate_pre) * up_pre).astype(low)
        activation_grad = contract_cols(upstream_parts[k], reduce_all[j])
        return activation, jnp.concatenate(swiglu_back(activation_grad, gate_pre, up_pre), 1)

    def mixed_back(parts, j):
        return contract_cols(parts[1], expand_all[j])

    def lowered(parts, j):
        return jnp.dot(parts[0], reduce_all[j], preferred_element_type=wide)

    done = {}
    grad_sums = {}

    def begin(k):
        done[k, 0] = hidden_part(k, 0)
        grad_sums[k] = mixed_back(done[k, 0], 0)

    def rest(k):
        for j in range(1, inner):
            done[k, j] = hidden_part(k, j)
            grad_sums[k] = grad_sums[k] + mixed_back(done[k, j], j)

    def summed(k):
        total = lowered(done[k, 0], 0)
        for j in range(1, inner):
            total = total + lowered(done[k, j], j)
        return total.astype(low) if k else total

    def joined(which, j):
        return jnp.concatenate([done[k, j][which] for k in range(outer)], 0)

    def expand_far(j):
        return contract_rows(mixed_near[:, D // 2 :], joined(1, j)).astype(low)

    def expand_term(j, x, far):
        rows = slice(x * D // head_devices, (x + 1) * D // head_devices)
        return contract_rows(mixed_near[:, rows], joined(1, j)) + far[rows].astype(wide)

    def reduce_far(j):
        return contract_rows(joined(0, j), upstream_near[:, D // 2 :]).astype(low)

    def reduce_term(j, x, far):
        columns = slice(x * D // head_devices, (x + 1) * D // head_devices)
        return contract_rows(joined(0, j), upstream_near[:, columns]) + far[:, columns].astype(wide)

    def x_finish(term, j, far, moved):
        for step in range(1, x_size):
            total = term(j, (step + 1) % x_size, far) + moved.astype(wide)
            if step + 1 < x_size:
                moved = hop(total.astype(low), "x")
        return total

    mixed_parts = [mixed]
    moved = outer_shift(mixed, 1)
    begin(0)
    moved, done, grad_sums, reduce_pieces, upstream_parts = tie(
        moved, done, grad_sums, reduce_pieces, upstream_parts
    )
    reduce_all = reduce_all + [reduce_whole(piece) for piece in reduce_pieces[1:]]
    mixed_parts.append(moved)
    moved = outer_shift(moved, 1)
    begin(1)
    upstream_all = jnp.concatenate(upstream_parts, 0)
    moved, done, grad_sums, upstream_all = tie(moved, done, grad_sums, upstream_all)
    mixed_parts.append(moved)
    moved = outer_shift(moved, 1)
    begin(2)
    rest(1)
    moved, done, grad_sums = tie(moved, done, grad_sums)
    mixed_parts.append(moved)
    moved = outer_shift(grad_sums[1].astype(low), 1)
    rest(2)
    begin(3)
    mixed_all = jnp.concatenate(mixed_parts, 0)
    moved, done, grad_sums, mixed_all, mixed_parts = tie(
        moved, done, grad_sums, mixed_all, mixed_parts
    )
    moved = outer_shift((grad_sums[2] + moved.astype(wide)).astype(low), 1)
    rest(3)
    rest(0)
    moved, done, grad_sums, mixed_all, upstream_all = tie(
        moved, done, grad_sums, mixed_all, upstream_all
    )
    moved = outer_shift((grad_sums[3] + moved.astype(wide)).astype(low), 1)
    late = range(1, inner)
    mixed_near = near_columns(mixed_all)
    expand_fars = [None] + [expand_far(j) for j in late]
    output_sums = {1: summed(1)}
    expand_own = contract_rows(mixed_all, joined(1, 0)).astype(low)
    moved, done, mixed_near, expand_fars, output_sums, expand_own, upstream_all = tie(
        moved, done, mixed_near, expand_fars, output_sums, expand_own, upstream_all
    )
    mixed_grad = grad_sums[0] + moved.astype(wide)
    _, second_back = jax.vjp(norm_rows, residual, norm_two)
    residual_from, two_grad = second_back(mixed_grad)
    residual_grad = upstream + residual_from
    residual_row = ring_gather(residual_grad.astype(low), "x")
    output_total = outer_shift(output_sums[1], 1)
    expand_fars = [None] + [swapped(expand_fars[j], "c", 1) for j in late]
    expand_lead = [None] + [
        expand_term(j, 1 % x_size, expand_fars[j]).astype(low) for j in late
    ]
    upstream_near = near_columns(upstream_all)
    reduce_fars = [None] + [reduce_far(j) for j in late]
    output_sums[2] = summed(2)
    output_sums[3] = summed(3)
    residual_row, output_total, expand_fars, expand_lead, reduce_fars, done, output_sums = tie(
        residual_row, output_total, expand_fars, expand_lead, reduce_fars, done, output_sums
    )
    residual_far = [swapped(piece, "c", 1) for piece in residual_row]
    reduce_fars = [None] + [swapped(reduce_fars[j], "c", 1) for j in late]
    gate_moved = [hop(expand_lead[j][:, :hidden], "x") for j in late]
    up_moved = [hop(expand_lead[j][:, hidden:], "x") for j in late]
    residual_all = jnp.concatenate(residual_row + residual_far, 0)
    residual_all, reduce_fars, done = tie(residual_all, reduce_fars, done)
    slots = wide_slots()

    def wide_parts(whole, axis, i):
        return [lax.dynamic_slice_in_dim(whole, slot * depth, depth, axis) for slot in slots[i]]

    order = [(step + 1) % outer for step in range(outer)]

    def output_rows_of(i):
        return jnp.concatenate(wide_parts(output_grad, 1, i), 1)

    gated_grad = contract_cols(residual_all, output_all)
    output_total = outer_shift(output_sums[2] + output_total, 1)
    back = attend_back(
        near,
        gated_grad,
        raw,
        starts[1],
        cosine,
        sine,
        head_gains,
        (query, key, value, attended, total_log),
        heads,
        groups,
    )
    back, output_total, done, residual_all, gate_moved, expand_own, upstream_all = tie(
        back, output_total, done, residual_all, gate_moved, expand_own, upstream_all
    )
    expand_own = lax.psum_scatter(expand_own, ("x", "c"), scatter_dimension=0, tiled=True)
    low_grads, low_near, head_gain_grads = back

    def normed_back(rows):
        return contract_cols(rows, project_all)

    project_grad = pinned(contract_rows(group_in, low_grads))
    project_grad, low_near, done, upstream_all, residual_all, gate_moved, reduce_fars, output_total = tie(
        project_grad, low_near, done, upstream_all, residual_all, gate_moved, reduce_fars, output_total
    )
    expand_moved = [None] + [jnp.concatenate(pair, 1) for pair in zip(gate_moved, up_moved)]
    output_total = outer_shift(output_sums[3] + output_total, 1)

    def spread(parts):
        total = parts[0]
        for part in parts[1:]:
            total = (part.astype(wide) + wide_from(total, 0, 1).astype(wide)).astype(low)
        return wide_from(total, 0, 1)

    project_total = inner_scatter(wide_parts(project_grad, 0, order[0]))
    output_grad = contract_rows(gated_near, residual_all)
    output_part = output_rows_of(order[0])
    expand_wide = [
        x_finish(expand_term, j, expand_fars[j], expand_moved[j]) for j in late
    ]
    reduce_lead = [None] + [
        reduce_term(j, 1 % x_size, reduce_fars[j]).astype(low) for j in late
    ]
    middle = len(expand_wide[0]) // 2
    expand_early = [part[:middle].astype(low) for part in expand_wide]
    expand_late = [part[middle:].astype(low) for part in expand_wide]
    normed_far = normed_back(low_near[half:]).astype(low)
    state = (project_total, output_part, output_grad, expand_early, expand_late, reduce_lead)
    state, project_grad, low_near, done, upstream_all, normed_far, output_total = tie(
        state, project_grad, low_near, done, upstream_all, normed_far, output_total
    )
    project_total, output_part, output_grad, expand_early, expand_late, reduce_lead = state
    for step, i in enumerate(order[1:]):
        moved = outer_shift(project_total.astype(low), 1)
        across = inner_scatter(wide_parts(project_grad, 0, i))
        if step == 0:
            normed_far = swapped(normed_far, "c", 1)
            normed_far, output_part = tie(normed_far, output_part)
        output_new = outer_shift(output_part.astype(low), 1)
        if step == 0:
            reduce_moved = [None] + [hop(reduce_lead[j], "x") for j in late]
            expand_early = spread(expand_early)
            normed_parts = []
            width = half // x_size
            for x in range(x_size):
                block = slice(x * width, (x + 1) * width)
                part = normed_back(low_near[block]) + normed_far[block].astype(wide)
                normed_parts.append(part.astype(low) if x == 1 else part)
            reduce_own = contract_rows(joined(0, 0), upstream_all).astype(low)
            reduce_wide = ()
        if step == 1:
            reduce_own = lax.psum_scatter(reduce_own, ("x", "c"), scatter_dimension=1, tiled=True)
            normed_moved = hop(normed_parts[1 % x_size], "x")
            expand_late = spread(expand_late)
            reduce_wide = [
                x_finish(reduce_term, j, reduce_fars[j], reduce_moved[j]).astype(low) for j in late
            ]
        if step == 2:
            reduce_wide = spread(reduce_wide)
        state = (moved, across, project_grad, output_new, output_grad, reduce_wide)
        if step == 0:
            state, expand_early, reduce_own, reduce_moved, expand_late, normed_parts = tie(
                state, expand_early, reduce_own, reduce_moved, expand_late, normed_parts
            )
        elif step == 1:
            state, expand_own, expand_late = tie(state, expand_own, expand_late)
        else:
            state, normed_moved, normed_parts = tie(state, normed_moved, normed_parts)
        moved, across, project_grad, output_new, output_grad, reduce_wide = state
        project_total = across + moved.astype(wide)
        output_part = output_rows_of(i) + output_new.astype(wide)
    output_part = inner_scatter([output_part[:, j * depth : (j + 1) * depth] for j in range(inner)])
    for step in range(1, x_size):
        normed_grad = normed_parts[(step + 1) % x_size] + normed_moved.astype(wide)
        if step + 1 < x_size:
            normed_moved = hop(normed_grad.astype(low), "x")
    expand_both = jnp.concatenate([expand_early, expand_late], 0).astype(wide)
    expand_both = expand_both + expand_own.astype(wide)
    reduce_part = reduce_wide.astype(wide) + reduce_own.astype(wide)
    project_part = pinned(project_total)
    block_output = (residual + summed(0) + output_total.astype(wide)).astype(low)
    _, first_back = jax.vjp(norm_rows, inputs, norm_one)
    input_from, one_grad = first_back(normed_grad)
    input_grad = residual_grad + input_from
    expand_part = jnp.stack([expand_both[:, :hidden], expand_both[:, hidden:]])
    query_part = project_part[:, :query_width]
    keyvalue_part = jnp.stack(
        [project_part[:, query_width:value_from], project_part[:, value_from:gate_from]]
    )
    headgate_part = pinned(project_part[:, gate_from : gate_from + heads].T)
    gain_partial = jnp.concatenate([one_grad, two_grad, head_gain_grads.reshape(-1)])
    parts = (query_part, keyvalue_part, headgate_part, output_part, expand_part, reduce_part)
    squares = jnp.zeros((), jnp.float32)
    for part_grad in parts:
        squares = squares + jnp.sum(part_grad * part_grad)
    totals = jnp.concatenate([gain_partial, squares[None]])
    totals = all_sum(totals)
    gains_grad, square_total = totals[:-1], totals[-1]
    grad_norm = jnp.sqrt(square_total + jnp.sum(gains_grad * gains_grad))
    clip = CLIP_NORM / jnp.maximum(grad_norm, CLIP_NORM)
    gains_new = adam_step(gains, gains_grad * clip, gain_first, gain_second, GAIN_RATE, 0.0)
    masters = (
        query_weight,
        keyvalue_weight,
        headgate_weight.T,
        output_weight,
        expand_weight,
        reduce_weight,
    )
    states = (
        (query_first, query_second),
        (keyvalue_first, keyvalue_second),
        (headgate_first.T, headgate_second.T),
        (output_first, output_second),
        (expand_first, expand_second),
        (reduce_first, reduce_second),
    )
    results = [grad_norm, block_output, input_grad, gains_new[0], gains_new[1], gains_new[2]]
    for index in range(6):
        rate = OUTPUT_RATE if index == 3 else WEIGHT_RATE
        updated, first_new, second_new = adam_step(
            masters[index],
            parts[index] * clip,
            states[index][0],
            states[index][1],
            rate,
            WEIGHT_DECAY,
        )
        made = [updated, first_new, second_new, updated.astype(low)]
        results = results + ([item.T for item in made] if index == 2 else made)
    return tuple(results)


def solution(mesh):
    heads, wides = mesh.shape["head"], mesh.shape["wide"]
    grid = Mesh(mesh.devices.reshape(heads // 2, 2, wides), ("x", "c", "w"))
    wide, head = ("w",), ("x", "c")
    rows = P(wide + head, None)
    by_wide = P(wide, head)
    stacked = P(None, wide, head)
    by_head = P(head, wide)
    widened = P(None, head, wide)
    return jax.shard_map(
        body,
        mesh=grid,
        in_specs=(rows, rows, P(wide), P(wide + head))
        + (P(),) * 4
        + (by_wide,) * 3
        + (stacked,) * 3
        + (by_wide,) * 3
        + (by_head,) * 3
        + (widened,) * 3
        + (by_wide,) * 3,
        out_specs=(P(), rows, rows)
        + (P(),) * 3
        + (by_wide,) * 4
        + (stacked,) * 4
        + (by_wide,) * 4
        + (by_head,) * 4
        + (widened,) * 4
        + (by_wide,) * 4,
        check_vma=False,
    )
```
